32 devices in a mesh: batch: 1, blk: 4 (over x, core), box: 8 (over z, y).
Axes of the slice: x: 2, y: 2, z: 4, core: 2. Of those that a mesh axis runs over, the one named last changes fastest.
Arguments:
- surface_points: float32 [3, 4096], P(None, ('blk', 'box')), may hold values from -4 to 4
- angle_ids: int32 [128], P('batch'), may hold values from 0 to 16383
- near_mask: int32 [32, 8], P(('blk', 'box')), may hold values 0 or 1
- skeleton: int32 [32, 32], P(('blk', 'box')), may hold values from 0 to 127, as said below
- box_inverse_parts: float32 [32, 2, 128, 128], P(('blk', 'box')), may hold values from -0.375 to 0.375
- near_coupling: float32 [32, 8, 2, 32, 128], P(('blk', 'box')), may hold values from -0.25 to 0.25
- top_inverse: float32 [4, 2, 256, 256], P('blk', None, 'box'), may hold values from -0.25 to 0.25
Outputs:
- scattered: float32 [2, 128, 4096], P(None, ('batch', 'box'), 'blk')
The draws below stay inside these ranges and needn't reach their ends.
Inputs may be any that keep to these rules, and one draw needn't show every extreme that they name: `skeleton`: each row holds 32 distinct row numbers of a box.
All inputs are finite; a program needn't handle non-finite values. No bound on the sum of `near_mask` on one device may be relied on, other than what follows from the above.
Results may differ from the reference program's by a relative error of at most 0.0003.
Values sent between devices are 32-bit elements; how exact they have to be, the bound alone decides.
A program may use at most 64 MiB of HBM per device.

```python
import jax
import jax.numpy as jnp
from jax import lax

B = 128
SKELETON_COUNT = 32
SWEEP = 16384
ANGLE_COUNT = 128
Q = 8
BOX_TOTAL = 32
NPTS = 4096
SK = 256
N_BLK = 4


def draw_skeleton(key, part):
    scores = jax.random.randint(jax.random.fold_in(key, 7), (BOX_TOTAL, B), 0, 1 << 20) * B + jnp.arange(B, dtype=jnp.int32)[None, :]
    order = jnp.argsort(scores, axis=1, stable=True)
    return order[:, :SKELETON_COUNT].astype(jnp.int32)


def set_ends(drawn, key, low, largest):
    extent = drawn.shape
    place = [jax.random.randint(jax.random.fold_in(key, axis), (), 0, extent[axis]) for axis in range(len(extent))]
    drawn = drawn.at[tuple(place)].set(low)
    longest = extent.index(max(extent))
    place[longest] = (place[longest] + 1) % extent[longest]
    return drawn.at[tuple(place)].set(largest)


def level_of(key, dims, shards, low, top_value):
    level = 1.0
    for axis_at, shards_of in shards:
        heights = jax.random.uniform(jax.random.fold_in(jax.random.fold_in(key, 6), axis_at), (shards_of,), jnp.float32, low / len(shards), top_value / len(shards))
        level = level * jnp.repeat(jnp.exp(heights), dims[axis_at] // shards_of).reshape((-1,) + (1,) * (len(dims) - 1 - axis_at))
    return level


def bell_draw(own_key, extent, scale, bound, shards=(), kind=jnp.bfloat16):
    array = jax.random.normal(own_key, extent, jnp.float32) * scale
    if len(shards) > 0:
        array = level_of(own_key, extent, shards, -0.22, 0.18) * array
    return jnp.clip(array, min=-bound, max=bound).astype(kind)


def setup_inputs(seed: int = 0, part: int = 0) -> dict:
    keys = jax.random.split(jax.random.key(seed), 8)
    own_keys = jax.random.split(jax.random.fold_in(keys[7], part), 8)
    surface_points = jnp.clip(jax.random.uniform(keys[0], (3, NPTS), jnp.float32, -4.0, 4.0) * level_of(keys[0], (3, NPTS), ((1, 32),), -0.4, 0.0), -4.0, 4.0)
    angle_ids = set_ends(jax.random.randint(own_keys[1], (ANGLE_COUNT,), 0, SWEEP), jax.random.fold_in(own_keys[1], 1), 0, SWEEP - 1).astype(jnp.int32)
    near_mask = set_ends((jax.random.randint(keys[2], (BOX_TOTAL, 8), 0, 4) < 3).astype(jnp.int32), jax.random.fold_in(keys[2], 1), 0, 1)
    skeleton = draw_skeleton(jax.random.fold_in(keys[7], 71), part)
    box_inverse_parts = bell_draw(keys[4], (BOX_TOTAL, 2, B, B), (2 * B) ** -0.5, 0.375, ((0, 32),), jnp.float32)
    near_coupling = bell_draw(keys[5], (BOX_TOTAL, 8, 2, SKELETON_COUNT, B), (16 * SKELETON_COUNT) ** -0.5, 0.25, ((0, 32),), jnp.float32)
    top_inverse = bell_draw(keys[6], (N_BLK, 2, SK, SK), (2 * SK) ** -0.5, 0.25, ((0, 4), (2, 8)), jnp.float32)
    return {"surface_points": surface_points, "angle_ids": angle_ids, "near_mask": near_mask, "skeleton": skeleton, "box_inverse_parts": box_inverse_parts, "near_coupling": near_coupling, "top_inverse": top_inverse}


wavenumber = 24.0
offsets = ((-1, -1), (-1, 0), (-1, 1), (0, -1), (0, 1), (1, -1), (1, 0), (1, 1))


def incident(points, angles):
    theta = angles.astype(jnp.float32) * (2.0 * jnp.pi / SWEEP)
    phase = wavenumber * (points[0][:, None] * jnp.cos(theta)[None, :] + points[1][:, None] * (0.6 * jnp.sin(theta))[None, :] + points[2][:, None] * (0.8 * jnp.sin(theta))[None, :])
    return jnp.stack([jnp.cos(phase), jnp.sin(phase)])


def complex_multiply(form, mat_re, mat_im, vec_re, vec_im):
    first = jnp.einsum(form, mat_re, vec_re, precision=lax.Precision.HIGHEST) - jnp.einsum(form, mat_im, vec_im, precision=lax.Precision.HIGHEST)
    second = jnp.einsum(form, mat_re, vec_im, precision=lax.Precision.HIGHEST) + jnp.einsum(form, mat_im, vec_re, precision=lax.Precision.HIGHEST)
    return first, second


def reference(surface_points, angle_ids, near_mask, skeleton, box_inverse_parts, near_coupling, top_inverse):
    field = incident(surface_points, angle_ids).reshape(2, BOX_TOTAL, B, ANGLE_COUNT)
    zre, zim = complex_multiply("brc,bca->bra", box_inverse_parts[:, 0], box_inverse_parts[:, 1], field[0], field[1])
    picker = jnp.broadcast_to(skeleton[:, :, None], (BOX_TOTAL, SKELETON_COUNT, ANGLE_COUNT))
    sre = jnp.take_along_axis(zre, picker, axis=1).reshape(N_BLK, Q, SKELETON_COUNT, ANGLE_COUNT)
    sim = jnp.take_along_axis(zim, picker, axis=1).reshape(N_BLK, Q, SKELETON_COUNT, ANGLE_COUNT)
    weights = near_coupling * near_mask.astype(jnp.float32)[:, :, None, None, None]
    weights = weights.reshape(N_BLK, Q, 8, 2, SKELETON_COUNT, B)
    cre = jnp.zeros((N_BLK, Q, B, ANGLE_COUNT), jnp.float32)
    cim = jnp.zeros((N_BLK, Q, B, ANGLE_COUNT), jnp.float32)
    for number, (step_s, step_q) in enumerate(offsets):
        near_re = jnp.roll(sre, (-step_s, -step_q), axis=(0, 1))
        near_im = jnp.roll(sim, (-step_s, -step_q), axis=(0, 1))
        term_re, term_im = complex_multiply("sqkr,sqka->sqra", weights[:, :, number, 0], weights[:, :, number, 1], near_re, near_im)
        cre = cre + term_re
        cim = cim + term_im
    weight_real = zre - cre.reshape(BOX_TOTAL, B, ANGLE_COUNT)
    wim = zim - cim.reshape(BOX_TOTAL, B, ANGLE_COUNT)
    tre = jnp.take_along_axis(weight_real, picker, axis=1).reshape(N_BLK, SK, ANGLE_COUNT)
    tim = jnp.take_along_axis(wim, picker, axis=1).reshape(N_BLK, SK, ANGLE_COUNT)
    output_real, yim = complex_multiply("src,sca->sra", top_inverse[:, 0], top_inverse[:, 1], tre, tim)
    one_hot_picker = (skeleton[:, :, None] == jnp.arange(B)[None, None, :]).astype(jnp.float32)
    vector_real = weight_real + jnp.einsum("wtj,wtc->wjc", one_hot_picker, output_real.reshape(BOX_TOTAL, SKELETON_COUNT, ANGLE_COUNT), precision=lax.Precision.HIGHEST)
    vector_imaginary = wim + jnp.einsum("wtj,wtc->wjc", one_hot_picker, yim.reshape(BOX_TOTAL, SKELETON_COUNT, ANGLE_COUNT), precision=lax.Precision.HIGHEST)
    solution_real, solution_imaginary = complex_multiply("vfd,vfg->vdg", box_inverse_parts[:, 0], box_inverse_parts[:, 1], vector_real, vector_imaginary)
    result = jnp.stack([solution_real.reshape(NPTS, ANGLE_COUNT), solution_imaginary.reshape(NPTS, ANGLE_COUNT)])
    return jnp.transpose(result, (0, 2, 1))
```

```python
import functools

import jax
import jax.numpy as jnp
from jax import lax
from jax.experimental import pallas as pl
from jax.experimental.pallas import tpu as pltpu
from jax.sharding import PartitionSpec as P

SWEEP = 16384
WAVENUMBER = 24.0
OFFSETS = ((-1, -1), (-1, 0), (-1, 1), (0, -1), (0, 1), (1, -1), (1, 0), (1, 1))
MESH = pl.DeviceIdType.MESH
F32 = jnp.float32
BF16 = jnp.bfloat16


def sin_cos(x):
    n = jnp.round(x * (2.0 / jnp.pi))
    r = x - n * 1.5703125
    r = r - n * 4.8375129699707031e-4
    r = r - n * 7.5497899548918822e-8
    s = r * r
    sine = ((-1.9515295891e-4 * s + 8.3321608736e-3) * s - 1.6666654611e-1) * s * r + r
    cosine = ((2.443315711809948e-5 * s - 1.388731625493765e-3) * s + 4.166664568298827e-2) * (
        s * s
    ) + (1.0 - 0.5 * s)
    place = n - 4.0 * jnp.floor(n * 0.25)
    odd = (place == 1.0) | (place == 3.0)
    sin_sign = jnp.where(place >= 2.0, -1.0, 1.0)
    cos_sign = jnp.where((place == 1.0) | (place == 2.0), -1.0, 1.0)
    return sin_sign * jnp.where(odd, cosine, sine), cos_sign * jnp.where(odd, sine, cosine)


def split(x):
    high = x.astype(BF16)
    return high, (x - high.astype(F32)).astype(BF16)


def dot(a, b):
    return jnp.dot(a, b, preferred_element_type=F32)


def dot3(a, b):
    return dot(a[0], b[0]) + (dot(a[0], b[1]) + dot(a[1], b[0]))


def beside(a, b, axis):
    return tuple(jnp.concatenate([a[i], b[i]], axis=axis) for i in range(2))


def kernel(
    n_blk,
    n_box,
    points_hbm,
    angles_hbm,
    mask_hbm,
    skeleton_hbm,
    l_hbm,
    e_hbm,
    g_hbm,
    out_ref,
    points_ref,
    angles_ref,
    mask_ref,
    skeleton_ref,
    l_ref,
    e_ref,
    g_ref,
    u_ref,
    near_ref,
    t_ref,
    x_ref,
    load_sem,
    u_send,
    u_recv,
    t_send,
    t_recv,
    x_send,
    x_recv,
):
    r = lax.axis_index("blk")
    q = lax.axis_index("box")
    width = l_ref.shape[1]
    rank = u_ref.shape[1]
    count = u_ref.shape[2]
    share = count // n_box

    def around(dr, dq):
        return {"blk": lax.rem(r + dr + n_blk, n_blk), "box": lax.rem(q + dq + n_box, n_box)}

    loads = [
        pltpu.make_async_copy(angles_hbm, angles_ref, load_sem.at[0]),
        pltpu.make_async_copy(points_hbm, points_ref, load_sem.at[1]),
        pltpu.make_async_copy(l_hbm.at[0], l_ref, load_sem.at[2]),
        pltpu.make_async_copy(e_hbm.at[0], e_ref, load_sem.at[3]),
        pltpu.make_async_copy(skeleton_hbm, skeleton_ref, load_sem.at[5]),
        pltpu.make_async_copy(mask_hbm, mask_ref, load_sem.at[6]),
        pltpu.make_async_copy(g_hbm.at[0], g_ref, load_sem.at[4]),
    ]
    for load in loads:
        load.start()

    barrier = pltpu.get_barrier_semaphore()
    greeted = [around(0, d) for d in range(1, n_box)]
    greeted += [around(dr, dq) for dr, dq in OFFSETS if dr != 0]
    for device in greeted:
        pl.semaphore_signal(barrier, inc=1, device_id=device, device_id_type=MESH)

    loads[0].wait()
    loads[1].wait()
    theta = angles_ref[...].astype(F32) * (2.0 * jnp.pi / SWEEP)
    sin_theta, cos_theta = sin_cos(theta)

    def column(i):
        return jnp.broadcast_to(points_ref[i : i + 1, :], (count, width)).T

    phase = WAVENUMBER * (
        column(0) * cos_theta + column(1) * (0.6 * sin_theta) + column(2) * (0.8 * sin_theta)
    )
    sine, cosine = sin_cos(phase)

    half = count // 2
    first = lax.broadcasted_iota(jnp.int32, (1, count), 1) < half

    def turned(a):
        return jnp.where(first, -1.0, 1.0) * pltpu.roll(a, half, 1)

    def both(a):
        return split(jnp.concatenate([a, turned(a)], axis=0))

    def both_transposed(a):
        return split(jnp.concatenate([a.T, turned(a).T], axis=1))

    field = [
        both(jnp.where(first, cosine, pltpu.roll(sine, half, 1))),
        both(jnp.where(first, pltpu.roll(cosine, half, 1), sine)),
    ]

    loads[4].wait()
    row = lax.broadcasted_iota(jnp.int32, (rank, width), 0)
    lane = lax.broadcasted_iota(jnp.int32, (rank, width), 1)
    wanted = jnp.zeros((rank, width), jnp.int32)
    for k in range(rank):
        wanted = jnp.where(row == k, skeleton_ref[0, k], wanted)
    picker = jnp.where(wanted == lane, 1.0, 0.0).astype(BF16)

    def pick(a):
        return tuple(dot(picker, half).astype(BF16) for half in a)

    loads[2].wait()
    lr, li = split(l_ref[0]), split(l_ref[1])
    plr, pli = pick(lr), pick(li)
    picked = beside(plr, pli, 1)
    u = [dot3(picked, part) for part in field]
    for h in range(2):
        u_ref[h] = u[h]

    pl.semaphore_wait(barrier, len(greeted))

    u_copies = [[], []]
    for h in range(2):
        for m, (dr, dq) in enumerate(OFFSETS):
            copy = pltpu.make_async_remote_copy(
                src_ref=u_ref.at[h],
                dst_ref=near_ref.at[h, 7 - m],
                send_sem=u_send.at[h, m],
                recv_sem=u_recv.at[h, 7 - m],
                device_id=around(dr, dq),
                device_id_type=MESH,
            )
            copy.start()
            u_copies[h].append(copy)

    whole = beside(lr, li, 1)
    z = [dot3(whole, part) for part in field]
    loads[3].wait()
    loads[5].wait()
    masked = [
        e_ref[m] * mask_ref[0, m].astype(F32) for m in range(len(OFFSETS))
    ]
    er = split(jnp.concatenate([e[0] for e in masked], axis=0).T)
    ei = split(jnp.concatenate([e[1] for e in masked], axis=0).T)
    coupling = beside(er, ei, 1)
    picked_coupling = beside(pick(er), pick(ei), 1)
    loads[6].wait()
    top = beside(split(g_ref[0]), split(g_ref[1]), 1)

    t_copies = [[], []]
    near = []
    for h in range(2):
        for copy in u_copies[h]:
            copy.wait_recv()
        near.append(both(near_ref[h].reshape(len(OFFSETS) * rank, count)))
        t_ref[h, pl.ds(q, 1)] = (u[h] - dot3(picked_coupling, near[h])).reshape(1, rank, count)
        for d in range(1, n_box):
            copy = pltpu.make_async_remote_copy(
                src_ref=t_ref.at[h, q],
                dst_ref=t_ref.at[h, q],
                send_sem=t_send.at[h, d],
                recv_sem=t_recv.at[h, d],
                device_id=around(0, d),
                device_id_type=MESH,
            )
            copy.start()
            t_copies[h].append(copy)

    below = beside(lr, li, 0)
    picked_below = beside(plr, pli, 0)
    x = [
        dot3(both_transposed(z[h] - dot3(coupling, near[h])), below) for h in range(2)
    ]

    here = pl.ds(pl.multiple_of(q * width, width), width)
    places = n_box // 2

    def send_x(to):
        d = lax.rem(to - q + n_box, n_box)
        return pltpu.make_async_remote_copy(
            src_ref=x_ref.at[to // places, :, pl.ds(to % places * share, share)],
            dst_ref=out_ref.at[:, :, here],
            send_sem=x_send.at[to],
            recv_sem=x_recv.at[d],
            device_id={"blk": r, "box": to},
            device_id_type=MESH,
        )

    for h in range(2):
        for copy in t_copies[h]:
            copy.wait_recv()
        y = dot3(top, both(t_ref[h].reshape(n_box * rank, count)))
        x_ref[h] = (x[h] + dot3(both_transposed(y), picked_below)).reshape(2, half, width)
        for to in range(h * places, h * places + places):

            @pl.when(q != to)
            def _(to=to):
                send_x(to).start()

    start = pl.multiple_of(lax.rem(q, places) * share, share)
    out_ref[:, :, here] = x_ref[q // places, :, pl.ds(start, share)]

    for d in range(1, n_box):
        pltpu.make_async_remote_copy(
            src_ref=x_ref.at[0, :, pl.ds(0, share)],
            dst_ref=out_ref.at[:, :, pl.ds(pl.multiple_of(lax.rem(q - d + n_box, n_box) * width, width), width)],
            send_sem=x_send.at[0],
            recv_sem=x_recv.at[d],
            device_id=around(0, d),
            device_id_type=MESH,
        ).wait_recv()
    for copy in u_copies[0] + u_copies[1] + t_copies[0] + t_copies[1]:
        copy.wait_send()
    for to in range(n_box):

        @pl.when(q != to)
        def _(to=to):
            send_x(to).wait_send()


def on_device(
    n_blk,
    n_box,
    surface_points,
    angle_ids,
    near_mask,
    skeleton,
    box_inverse_parts,
    near_coupling,
    top_inverse,
):
    width = box_inverse_parts.shape[2]
    count = angle_ids.shape[0]
    rank = skeleton.shape[1]
    vmem = pl.BlockSpec(memory_space=pltpu.VMEM)
    hbm = pl.BlockSpec(memory_space=pl.ANY)
    return pl.pallas_call(
        functools.partial(kernel, n_blk, n_box),
        out_shape=jax.ShapeDtypeStruct((2, count // n_box, n_box * width), F32),
        in_specs=[hbm] * 7,
        out_specs=vmem,
        scratch_shapes=[
            pltpu.VMEM(surface_points.shape, F32),
            pltpu.VMEM((1, count), jnp.int32),
            pltpu.SMEM(near_mask.shape, jnp.int32),
            pltpu.SMEM(skeleton.shape, jnp.int32),
            pltpu.VMEM(box_inverse_parts.shape[1:], F32),
            pltpu.VMEM(near_coupling.shape[1:], F32),
            pltpu.VMEM(top_inverse.shape[1:], F32),
            pltpu.VMEM((2, rank, count), F32),
            pltpu.VMEM((2, len(OFFSETS), rank, count), F32),
            pltpu.VMEM((2, n_box, rank, count), F32),
            pltpu.VMEM((2, 2, count // 2, width), F32),
            pltpu.SemaphoreType.DMA((7,)),
            pltpu.SemaphoreType.DMA((2, len(OFFSETS))),
            pltpu.SemaphoreType.DMA((2, len(OFFSETS))),
            pltpu.SemaphoreType.DMA((2, n_box)),
            pltpu.SemaphoreType.DMA((2, n_box)),
            pltpu.SemaphoreType.DMA((n_box,)),
            pltpu.SemaphoreType.DMA((n_box,)),
        ],
        compiler_params=pltpu.CompilerParams(
            collective_id=0, has_side_effects=True, vmem_limit_bytes=16 * 1024 * 1024
        ),
    )(
        *(
            pltpu.with_memory_space_constraint(a, pltpu.HBM)
            for a in (
                surface_points,
                angle_ids.reshape(1, count),
                near_mask,
                skeleton,
                box_inverse_parts,
                near_coupling,
                top_inverse,
            )
        )
    )


def solution(mesh):
    return jax.shard_map(
        functools.partial(on_device, mesh.shape["blk"], mesh.shape["box"]),
        mesh=mesh,
        in_specs=(
            P(None, ("blk", "box")),
            P("batch"),
            P(("blk", "box"), None),
            P(("blk", "box"), None),
            P(("blk", "box"), None, None, None),
            P(("blk", "box"), None, None, None, None),
            P("blk", None, "box", None),
        ),
        out_specs=P(None, ("batch", "box"), "blk"),
        check_vma=False,
    )
```

```python
import functools

import jax
import jax.numpy as jnp
from jax import lax
from jax.experimental import pallas as pl
from jax.experimental.pallas import tpu as pltpu
from jax.sharding import PartitionSpec as P

SWEEP = 16384
WAVENUMBER = 24.0
OFFSETS = ((-1, -1), (-1, 0), (-1, 1), (0, -1), (0, 1), (1, -1), (1, 0), (1, 1))
MESH = pl.DeviceIdType.MESH
F32 = jnp.float32
BF16 = jnp.bfloat16


def sin_cos(x):
    n = jnp.round(x * (2.0 / jnp.pi))
    r = x - n * 1.5703125
    r = r - n * 4.8375129699707031e-4
    r = r - n * 7.5497899548918822e-8
    s = r * r
    sine = ((-1.9515295891e-4 * s + 8.3321608736e-3) * s - 1.6666654611e-1) * s * r + r
    cosine = ((2.443315711809948e-5 * s - 1.388731625493765e-3) * s + 4.166664568298827e-2) * (
        s * s
    ) + (1.0 - 0.5 * s)
    place = n - 4.0 * jnp.floor(n * 0.25)
    odd = (place == 1.0) | (place == 3.0)
    sin_sign = jnp.where(place >= 2.0, -1.0, 1.0)
    cos_sign = jnp.where((place == 1.0) | (place == 2.0), -1.0, 1.0)
    return sin_sign * jnp.where(odd, cosine, sine), cos_sign * jnp.where(odd, sine, cosine)


def split(x):
    high = x.astype(BF16)
    return high, (x - high.astype(F32)).astype(BF16)


def dot(a, b):
    return jnp.dot(a, b, preferred_element_type=F32)


def dot3(a, b):
    return dot(a[0], b[0]) + (dot(a[0], b[1]) + dot(a[1], b[0]))


def beside(a, b, axis):
    return tuple(jnp.concatenate([a[i], b[i]], axis=axis) for i in range(2))


def kernel(
    n_blk,
    n_box,
    points_hbm,
    angles_hbm,
    mask_hbm,
    skeleton_hbm,
    l_hbm,
    e_hbm,
    g_hbm,
    out_ref,
    points_ref,
    angles_ref,
    mask_ref,
    skeleton_ref,
    l_ref,
    e_ref,
    g_ref,
    u_ref,
    near_ref,
    t_ref,
    x_ref,
    load_sem,
    u_send,
    u_recv,
    t_send,
    t_recv,
    x_send,
    x_recv,
):
    r = lax.axis_index("blk")
    q = lax.axis_index("box")
    width = l_ref.shape[1]
    rank = u_ref.shape[1]
    count = u_ref.shape[2]
    share = count // n_box

    def around(dr, dq):
        return {"blk": lax.rem(r + dr + n_blk, n_blk), "box": lax.rem(q + dq + n_box, n_box)}

    def across(k):
        place = q
        bit = 1
        while bit <= k:
            if k & bit:
                place = place + bit - 2 * bit * lax.rem(q // bit, 2)
            bit *= 2
        return {"blk": r, "box": place}

    loads = [
        pltpu.make_async_copy(angles_hbm, angles_ref, load_sem.at[0]),
        pltpu.make_async_copy(points_hbm, points_ref, load_sem.at[1]),
        pltpu.make_async_copy(l_hbm.at[0], l_ref, load_sem.at[2]),
        pltpu.make_async_copy(e_hbm.at[0], e_ref, load_sem.at[3]),
        pltpu.make_async_copy(skeleton_hbm, skeleton_ref, load_sem.at[5]),
        pltpu.make_async_copy(mask_hbm, mask_ref, load_sem.at[6]),
        pltpu.make_async_copy(g_hbm.at[0], g_ref, load_sem.at[4]),
    ]
    for load in loads:
        load.start()

    barrier = pltpu.get_barrier_semaphore()
    greeted = [around(0, d) for d in range(1, n_box)]
    greeted += [around(dr, dq) for dr, dq in OFFSETS if dr != 0]
    for device in greeted:
        pl.semaphore_signal(barrier, inc=1, device_id=device, device_id_type=MESH)

    loads[0].wait()
    loads[1].wait()
    theta = angles_ref[...].astype(F32) * (2.0 * jnp.pi / SWEEP)
    sin_theta, cos_theta = sin_cos(theta)

    def column(i):
        return jnp.broadcast_to(points_ref[i : i + 1, :], (count, width)).T

    phase = WAVENUMBER * (
        column(0) * cos_theta + column(1) * (0.6 * sin_theta) + column(2) * (0.8 * sin_theta)
    )
    sine, cosine = sin_cos(phase)

    half = count // 2
    first = lax.broadcasted_iota(jnp.int32, (1, count), 1) < half

    def turned(a):
        return jnp.where(first, -1.0, 1.0) * pltpu.roll(a, half, 1)

    def both(a):
        return split(jnp.concatenate([a, turned(a)], axis=0))

    def both_transposed(a):
        return split(jnp.concatenate([a.T, turned(a).T], axis=1))

    field = [
        both(jnp.where(first, cosine, pltpu.roll(sine, half, 1))),
        both(jnp.where(first, pltpu.roll(cosine, half, 1), sine)),
    ]

    loads[4].wait()
    row = lax.broadcasted_iota(jnp.int32, (rank, width), 0)
    lane = lax.broadcasted_iota(jnp.int32, (rank, width), 1)
    wanted = jnp.zeros((rank, width), jnp.int32)
    for k in range(rank):
        wanted = jnp.where(row == k, skeleton_ref[0, k], wanted)
    picker = jnp.where(wanted == lane, 1.0, 0.0).astype(BF16)

    def pick(a):
        return tuple(dot(picker, half).astype(BF16) for half in a)

    loads[2].wait()
    lr, li = split(l_ref[0]), split(l_ref[1])
    plr, pli = pick(lr), pick(li)
    picked = beside(plr, pli, 1)
    u = [dot3(picked, part) for part in field]
    for h in range(2):
        u_ref[h] = u[h]

    pl.semaphore_wait(barrier, len(greeted))

    u_copies = [[], []]
    for h in range(2):
        for m, (dr, dq) in enumerate(OFFSETS):
            copy = pltpu.make_async_remote_copy(
                src_ref=u_ref.at[h],
                dst_ref=near_ref.at[h, 7 - m],
                send_sem=u_send.at[h, m],
                recv_sem=u_recv.at[h, 7 - m],
                device_id=around(dr, dq),
                device_id_type=MESH,
            )
            copy.start()
            u_copies[h].append(copy)

    whole = beside(lr, li, 1)
    z = [dot3(whole, part) for part in field]
    loads[3].wait()
    loads[5].wait()
    masked = [
        e_ref[m] * mask_ref[0, m].astype(F32) for m in range(len(OFFSETS))
    ]
    er = split(jnp.concatenate([e[0] for e in masked], axis=0).T)
    ei = split(jnp.concatenate([e[1] for e in masked], axis=0).T)
    coupling = beside(er, ei, 1)
    picked_coupling = beside(pick(er), pick(ei), 1)
    loads[6].wait()
    top = beside(split(g_ref[0]), split(g_ref[1]), 1)

    t_copies = [[], []]
    near = []
    for h in range(2):
        for copy in u_copies[h]:
            copy.wait_recv()
        near.append(both(near_ref[h].reshape(len(OFFSETS) * rank, count)))
        t_ref[h, pl.ds(q, 1)] = (u[h] - dot3(picked_coupling, near[h])).reshape(1, rank, count)
        for d in range(1, n_box):
            copy = pltpu.make_async_remote_copy(
                src_ref=t_ref.at[h, q],
                dst_ref=t_ref.at[h, q],
                send_sem=t_send.at[h, d],
                recv_sem=t_recv.at[h, d],
                device_id=across(d),
                device_id_type=MESH,
            )
            copy.start()
            t_copies[h].append(copy)

    below = beside(lr, li, 0)
    picked_below = beside(plr, pli, 0)
    x = [
        dot3(both_transposed(z[h] - dot3(coupling, near[h])), below) for h in range(2)
    ]

    here = pl.ds(pl.multiple_of(q * width, width), width)
    places = n_box // 2

    def send_x(to):
        d = lax.rem(to - q + n_box, n_box)
        return pltpu.make_async_remote_copy(
            src_ref=x_ref.at[to // places, :, pl.ds(to % places * share, share)],
            dst_ref=out_ref.at[:, :, here],
            send_sem=x_send.at[to],
            recv_sem=x_recv.at[d],
            device_id={"blk": r, "box": to},
            device_id_type=MESH,
        )

    for h in range(2):
        for copy in t_copies[h]:
            copy.wait_recv()
        y = dot3(top, both(t_ref[h].reshape(n_box * rank, count)))
        x_ref[h] = (x[h] + dot3(both_transposed(y), picked_below)).reshape(2, half, width)
        for to in range(h * places, h * places + places):

            @pl.when(q != to)
            def _(to=to):
                send_x(to).start()

    start = pl.multiple_of(lax.rem(q, places) * share, share)
    out_ref[:, :, here] = x_ref[q // places, :, pl.ds(start, share)]

    for d in range(1, n_box):
        pltpu.make_async_remote_copy(
            src_ref=x_ref.at[0, :, pl.ds(0, share)],
            dst_ref=out_ref.at[:, :, pl.ds(pl.multiple_of(lax.rem(q - d + n_box, n_box) * width, width), width)],
            send_sem=x_send.at[0],
            recv_sem=x_recv.at[d],
            device_id=around(0, d),
            device_id_type=MESH,
        ).wait_recv()
    for copy in u_copies[0] + u_copies[1] + t_copies[0] + t_copies[1]:
        copy.wait_send()
    for to in range(n_box):

        @pl.when(q != to)
        def _(to=to):
            send_x(to).wait_send()


def on_device(
    n_blk,
    n_box,
    surface_points,
    angle_ids,
    near_mask,
    skeleton,
    box_inverse_parts,
    near_coupling,
    top_inverse,
):
    width = box_inverse_parts.shape[2]
    count = angle_ids.shape[0]
    rank = skeleton.shape[1]
    vmem = pl.BlockSpec(memory_space=pltpu.VMEM)
    hbm = pl.BlockSpec(memory_space=pl.ANY)
    return pl.pallas_call(
        functools.partial(kernel, n_blk, n_box),
        out_shape=jax.ShapeDtypeStruct((2, count // n_box, n_box * width), F32),
        in_specs=[hbm] * 7,
        out_specs=vmem,
        scratch_shapes=[
            pltpu.VMEM(surface_points.shape, F32),
            pltpu.VMEM((1, count), jnp.int32),
            pltpu.SMEM(near_mask.shape, jnp.int32),
            pltpu.SMEM(skeleton.shape, jnp.int32),
            pltpu.VMEM(box_inverse_parts.shape[1:], F32),
            pltpu.VMEM(near_coupling.shape[1:], F32),
            pltpu.VMEM(top_inverse.shape[1:], F32),
            pltpu.VMEM((2, rank, count), F32),
            pltpu.VMEM((2, len(OFFSETS), rank, count), F32),
            pltpu.VMEM((2, n_box, rank, count), F32),
            pltpu.VMEM((2, 2, count // 2, width), F32),
            pltpu.SemaphoreType.DMA((7,)),
            pltpu.SemaphoreType.DMA((2, len(OFFSETS))),
            pltpu.SemaphoreType.DMA((2, len(OFFSETS))),
            pltpu.SemaphoreType.DMA((2, n_box)),
            pltpu.SemaphoreType.DMA((2, n_box)),
            pltpu.SemaphoreType.DMA((n_box,)),
            pltpu.SemaphoreType.DMA((n_box,)),
        ],
        compiler_params=pltpu.CompilerParams(
            collective_id=0, has_side_effects=True, vmem_limit_bytes=16 * 1024 * 1024
        ),
    )(
        *(
            pltpu.with_memory_space_constraint(a, pltpu.HBM)
            for a in (
                surface_points,
                angle_ids.reshape(1, count),
                near_mask,
                skeleton,
                box_inverse_parts,
                near_coupling,
                top_inverse,
            )
        )
    )


def solution(mesh):
    return jax.shard_map(
        functools.partial(on_device, mesh.shape["blk"], mesh.shape["box"]),
        mesh=mesh,
        in_specs=(
            P(None, ("blk", "box")),
            P("batch"),
            P(("blk", "box"), None),
            P(("blk", "box"), None),
            P(("blk", "box"), None, None, None),
            P(("blk", "box"), None, None, None, None),
            P("blk", None, "box", None),
        ),
        out_specs=P(None, ("batch", "box"), "blk"),
        check_vma=False,
    )
```

```python
import functools

import jax
import jax.numpy as jnp
from jax import lax
from jax.experimental import pallas as pl
from jax.experimental.pallas import tpu as pltpu
from jax.sharding import PartitionSpec as P

SWEEP = 16384
WAVENUMBER = 24.0
OFFSETS = ((-1, -1), (-1, 0), (-1, 1), (0, -1), (0, 1), (1, -1), (1, 0), (1, 1))
MESH = pl.DeviceIdType.MESH
F32 = jnp.float32
BF16 = jnp.bfloat16


def sin_cos(x):
    n = jnp.round(x * (2.0 / jnp.pi))
    r = x - n * 1.5703125
    r = r - n * 4.8375129699707031e-4
    r = r - n * 7.5497899548918822e-8
    s = r * r
    sine = ((-1.9515295891e-4 * s + 8.3321608736e-3) * s - 1.6666654611e-1) * s * r + r
    cosine = ((2.443315711809948e-5 * s - 1.388731625493765e-3) * s + 4.166664568298827e-2) * (
        s * s
    ) + (1.0 - 0.5 * s)
    place = n - 4.0 * jnp.floor(n * 0.25)
    odd = (place == 1.0) | (place == 3.0)
    sin_sign = jnp.where(place >= 2.0, -1.0, 1.0)
    cos_sign = jnp.where((place == 1.0) | (place == 2.0), -1.0, 1.0)
    return sin_sign * jnp.where(odd, cosine, sine), cos_sign * jnp.where(odd, sine, cosine)


def split(x):
    high = x.astype(BF16)
    return high, (x - high.astype(F32)).astype(BF16)


def dot(a, b):
    return jnp.dot(a, b, preferred_element_type=F32)


def dot3(a, b):
    return dot(a[0], b[0]) + (dot(a[0], b[1]) + dot(a[1], b[0]))


def beside(a, b, axis):
    return tuple(jnp.concatenate([a[i], b[i]], axis=axis) for i in range(2))


def kernel(
    n_blk,
    n_box,
    points_hbm,
    angles_hbm,
    mask_hbm,
    skeleton_hbm,
    l_hbm,
    e_hbm,
    g_hbm,
    out_ref,
    points_ref,
    angles_ref,
    mask_ref,
    skeleton_ref,
    l_ref,
    e_ref,
    g_ref,
    u_ref,
    near_ref,
    mine_ref,
    t_ref,
    p_ref,
    above_ref,
    other_ref,
    x_ref,
    came_ref,
    load_sem,
    u_send,
    u_recv,
    t_send,
    t_recv,
    pair_send,
    pair_recv,
    w_send,
    w_recv,
    x_send,
    x_recv,
):
    r = lax.axis_index("blk")
    q = lax.axis_index("box")
    width = l_ref.shape[1]
    rank = u_ref.shape[1]
    count = u_ref.shape[2]
    share = count // n_box
    half = count // 2
    pairs = n_box // 2
    pair = q // 2
    side = lax.rem(q, 2)

    def around(dr, dq):
        return {"blk": lax.rem(r + dr + n_blk, n_blk), "box": lax.rem(q + dq + n_box, n_box)}

    def across(k):
        place = q
        bit = 1
        while bit <= k:
            if k & bit:
                place = place + bit - 2 * bit * lax.rem(q // bit, 2)
            bit *= 2
        return {"blk": r, "box": place}

    loads = [
        pltpu.make_async_copy(angles_hbm, angles_ref, load_sem.at[0]),
        pltpu.make_async_copy(points_hbm, points_ref, load_sem.at[1]),
        pltpu.make_async_copy(l_hbm.at[0], l_ref, load_sem.at[2]),
        pltpu.make_async_copy(e_hbm.at[0], e_ref, load_sem.at[3]),
        pltpu.make_async_copy(skeleton_hbm, skeleton_ref, load_sem.at[5]),
        pltpu.make_async_copy(mask_hbm, mask_ref, load_sem.at[6]),
        pltpu.make_async_copy(g_hbm.at[0], g_ref.at[0], load_sem.at[4]),
    ]
    for load in loads:
        load.start()

    barrier = pltpu.get_barrier_semaphore()
    greeted = [around(0, d) for d in range(1, n_box)]
    greeted += [around(dr, dq) for dr, dq in OFFSETS if dr != 0]
    for device in greeted:
        pl.semaphore_signal(barrier, inc=1, device_id=device, device_id_type=MESH)

    loads[0].wait()
    loads[1].wait()
    given = angles_ref[...].astype(F32)
    block = lax.broadcasted_iota(jnp.int32, (1, count), 1) // share
    theta = given
    for j in range(n_box):
        source = 2 * j if j < pairs else 2 * (j - pairs) + 1
        if source != j:
            moved = pltpu.roll(given, (j - source) % n_box * share, 1)
            theta = jnp.where(block == j, moved, theta)
    theta = theta * (2.0 * jnp.pi / SWEEP)
    sin_theta, cos_theta = sin_cos(theta)

    def column(i):
        return jnp.broadcast_to(points_ref[i : i + 1, :], (count, width)).T

    phase = WAVENUMBER * (
        column(0) * cos_theta + column(1) * (0.6 * sin_theta) + column(2) * (0.8 * sin_theta)
    )
    sine, cosine = sin_cos(phase)

    first = lax.broadcasted_iota(jnp.int32, (1, count), 1) < half

    def turned(a):
        return jnp.where(first, -1.0, 1.0) * pltpu.roll(a, half, 1)

    def both(a):
        return split(jnp.concatenate([a, turned(a)], axis=0))

    def both_transposed(a):
        return split(jnp.concatenate([a.T, turned(a).T], axis=1))

    field = [
        both(jnp.where(first, cosine, pltpu.roll(sine, half, 1))),
        both(jnp.where(first, pltpu.roll(cosine, half, 1), sine)),
    ]

    loads[4].wait()
    row = lax.broadcasted_iota(jnp.int32, (rank, width), 0)
    lane = lax.broadcasted_iota(jnp.int32, (rank, width), 1)
    wanted = jnp.zeros((rank, width), jnp.int32)
    for k in range(rank):
        wanted = jnp.where(row == k, skeleton_ref[0, k], wanted)
    picker = jnp.where(wanted == lane, 1.0, 0.0).astype(BF16)

    def pick(a):
        return tuple(dot(picker, half).astype(BF16) for half in a)

    loads[2].wait()
    lr, li = split(l_ref[0]), split(l_ref[1])
    plr, pli = pick(lr), pick(li)
    picked = beside(plr, pli, 1)
    u = [dot3(picked, part) for part in field]
    for h in range(2):
        u_ref[h] = u[h]
    for i, part in enumerate((plr, pli)):
        p_ref[0, i] = part[0].astype(F32) + part[1].astype(F32)

    pl.semaphore_wait(barrier, len(greeted))

    u_copies = [[], []]
    for h in range(2):
        for m, (dr, dq) in enumerate(OFFSETS):
            copy = pltpu.make_async_remote_copy(
                src_ref=u_ref.at[h],
                dst_ref=near_ref.at[h, 7 - m],
                send_sem=u_send.at[h, m],
                recv_sem=u_recv.at[h, 7 - m],
                device_id=around(dr, dq),
                device_id_type=MESH,
            )
            copy.start()
            u_copies[h].append(copy)

    pair_copies = [
        pltpu.make_async_remote_copy(
            src_ref=ref.at[0],
            dst_ref=ref.at[1],
            send_sem=pair_send.at[i],
            recv_sem=pair_recv.at[i],
            device_id=across(1),
            device_id_type=MESH,
        )
        for i, ref in enumerate((g_ref, p_ref))
    ]
    loads[6].wait()
    for copy in pair_copies:
        copy.start()

    whole = beside(lr, li, 1)
    z = [dot3(whole, part) for part in field]
    loads[3].wait()
    loads[5].wait()
    masked = [
        e_ref[m] * mask_ref[0, m].astype(F32) for m in range(len(OFFSETS))
    ]
    er = split(jnp.concatenate([e[0] for e in masked], axis=0).T)
    ei = split(jnp.concatenate([e[1] for e in masked], axis=0).T)
    coupling = beside(er, ei, 1)
    picked_coupling = beside(pick(er), pick(ei), 1)

    def send_t(h, d):
        return pltpu.make_async_remote_copy(
            src_ref=mine_ref.at[h],
            dst_ref=t_ref.at[q],
            send_sem=t_send.at[d],
            recv_sem=t_recv.at[d],
            device_id=across(d),
            device_id_type=MESH,
        )

    near = []
    for h in range(2):
        for copy in u_copies[h]:
            copy.wait_recv()
        near.append(both(near_ref[h].reshape(len(OFFSETS) * rank, count)))
        mine_ref[h] = u[h] - dot3(picked_coupling, near[h])
        for d in range(1, n_box):

            @pl.when(lax.rem(q + d, 2) == h)
            def _(h=h, d=d):
                send_t(h, d).start()

    t_ref[pl.ds(q, 1)] = mine_ref[pl.ds(side, 1)]

    below = beside(lr, li, 0)
    for h in range(2):
        above_ref[h] = dot3(
            both_transposed(z[h] - dot3(coupling, near[h])), below
        ).reshape(2, half, width)

    def send_w(to):
        return pltpu.make_async_remote_copy(
            src_ref=above_ref.at[1 - side, :, pl.ds(to * share, share)],
            dst_ref=other_ref.at[pair],
            send_sem=w_send.at[to],
            recv_sem=w_recv.at[pair],
            device_id={"blk": r, "box": 2 * to + 1 - side},
            device_id_type=MESH,
        )

    for to in range(pairs):
        send_w(to).start()

    for copy in pair_copies:
        copy.wait_recv()
    top = split(
        jnp.concatenate(
            [
                jnp.concatenate([g_ref[i, 0], g_ref[i, 1]], axis=1)
                for i in range(2)
            ],
            axis=0,
        )
    )
    none = jnp.zeros((rank, width), F32)
    spread = split(
        jnp.concatenate(
            [
                jnp.concatenate([p_ref[0, c], none] if i == 0 else [none, p_ref[1, c]], axis=1)
                for c in range(2)
                for i in range(2)
            ],
            axis=0,
        )
    )

    for d in range(1, n_box):
        send_t(0, d).wait_recv()
    y = dot3(top, both(t_ref[...].reshape(n_box * rank, count)))
    x = dot3(both_transposed(y), spread)
    x_ref[0] = above_ref[side] + x[:, :width].reshape(2, half, width)
    x_ref[1] = x[:, width:].reshape(2, half, width)

    def send_x(to, here):
        return pltpu.make_async_remote_copy(
            src_ref=x_ref.at[:, :, pl.ds(to * share, share)],
            dst_ref=came_ref.at[here],
            send_sem=x_send.at[to],
            recv_sem=x_recv.at[here],
            device_id={"blk": r, "box": 2 * to + side},
            device_id_type=MESH,
        )

    for to in range(pairs):

        @pl.when(pair != to)
        def _(to=to):
            send_x(to, pair).start()

    def place(box):
        return pl.ds(pl.multiple_of(box * width, width), width)

    for here in range(pairs):
        pltpu.make_async_remote_copy(
            src_ref=above_ref.at[0, :, pl.ds(0, share)],
            dst_ref=other_ref.at[here],
            send_sem=w_send.at[here],
            recv_sem=w_recv.at[here],
            device_id=across(1),
            device_id_type=MESH,
        ).wait_recv()

    own = pl.ds(pl.multiple_of(pair * share, share), share)
    out_ref[:, :, place(q)] = x_ref[0, :, own]
    out_ref[:, :, place(2 * pair + 1 - side)] = x_ref[1, :, own] + other_ref[pair]

    for here in range(pairs):

        @pl.when(pair != here)
        def _(here=here):
            send_x(here, here).wait_recv()
            out_ref[:, :, place(2 * here + side)] = came_ref[here, 0]
            out_ref[:, :, place(2 * here + 1 - side)] = came_ref[here, 1] + other_ref[here]

    for copy in u_copies[0] + u_copies[1] + pair_copies:
        copy.wait_send()
    for d in range(1, n_box):
        send_t(0, d).wait_send()
    for to in range(pairs):
        send_w(to).wait_send()

        @pl.when(pair != to)
        def _(to=to):
            send_x(to, pair).wait_send()


def on_device(
    n_blk,
    n_box,
    surface_points,
    angle_ids,
    near_mask,
    skeleton,
    box_inverse_parts,
    near_coupling,
    top_inverse,
):
    width = box_inverse_parts.shape[2]
    count = angle_ids.shape[0]
    rank = skeleton.shape[1]
    vmem = pl.BlockSpec(memory_space=pltpu.VMEM)
    hbm = pl.BlockSpec(memory_space=pl.ANY)
    return pl.pallas_call(
        functools.partial(kernel, n_blk, n_box),
        out_shape=jax.ShapeDtypeStruct((2, count // n_box, n_box * width), F32),
        in_specs=[hbm] * 7,
        out_specs=vmem,
        scratch_shapes=[
            pltpu.VMEM(surface_points.shape, F32),
            pltpu.VMEM((1, count), jnp.int32),
            pltpu.SMEM(near_mask.shape, jnp.int32),
            pltpu.SMEM(skeleton.shape, jnp.int32),
            pltpu.VMEM(box_inverse_parts.shape[1:], F32),
            pltpu.VMEM(near_coupling.shape[1:], F32),
            pltpu.VMEM((2, *top_inverse.shape[1:]), F32),
            pltpu.VMEM((2, rank, count), F32),
            pltpu.VMEM((2, len(OFFSETS), rank, count), F32),
            pltpu.VMEM((2, rank, count), F32),
            pltpu.VMEM((n_box, rank, count), F32),
            pltpu.VMEM((2, 2, rank, width), F32),
            pltpu.VMEM((2, 2, count // 2, width), F32),
            pltpu.VMEM((n_box // 2, 2, count // n_box, width), F32),
            pltpu.VMEM((2, 2, count // 2, width), F32),
            pltpu.VMEM((n_box // 2, 2, 2, count // n_box, width), F32),
            pltpu.SemaphoreType.DMA((7,)),
            pltpu.SemaphoreType.DMA((2, len(OFFSETS))),
            pltpu.SemaphoreType.DMA((2, len(OFFSETS))),
            pltpu.SemaphoreType.DMA((n_box,)),
            pltpu.SemaphoreType.DMA((n_box,)),
            pltpu.SemaphoreType.DMA((2,)),
            pltpu.SemaphoreType.DMA((2,)),
            pltpu.SemaphoreType.DMA((n_box // 2,)),
            pltpu.SemaphoreType.DMA((n_box // 2,)),
            pltpu.SemaphoreType.DMA((n_box // 2,)),
            pltpu.SemaphoreType.DMA((n_box // 2,)),
        ],
        compiler_params=pltpu.CompilerParams(
            collective_id=0, has_side_effects=True, vmem_limit_bytes=16 * 1024 * 1024
        ),
    )(
        *(
            pltpu.with_memory_space_constraint(a, pltpu.HBM)
            for a in (
                surface_points,
                angle_ids.reshape(1, count),
                near_mask,
                skeleton,
                box_inverse_parts,
                near_coupling,
                top_inverse,
            )
        )
    )


def solution(mesh):
    return jax.shard_map(
        functools.partial(on_device, mesh.shape["blk"], mesh.shape["box"]),
        mesh=mesh,
        in_specs=(
            P(None, ("blk", "box")),
            P("batch"),
            P(("blk", "box"), None),
            P(("blk", "box"), None),
            P(("blk", "box"), None, None, None),
            P(("blk", "box"), None, None, None, None),
            P("blk", None, "box", None),
        ),
        out_specs=P(None, ("batch", "box"), "blk"),
        check_vma=False,
    )
```

```python
import functools

import jax
import jax.numpy as jnp
from jax import lax
from jax.experimental import pallas as pl
from jax.experimental.pallas import tpu as pltpu
from jax.sharding import PartitionSpec as P

SWEEP = 16384
WAVENUMBER = 24.0
OFFSETS = ((-1, -1), (-1, 0), (-1, 1), (0, -1), (0, 1), (1, -1), (1, 0), (1, 1))
MESH = pl.DeviceIdType.MESH
F32 = jnp.float32
BF16 = jnp.bfloat16


def sin_cos(x):
    n = jnp.round(x * (2.0 / jnp.pi))
    r = x - n * 1.5703125
    r = r - n * 4.8375129699707031e-4
    r = r - n * 7.5497899548918822e-8
    s = r * r
    sine = ((-1.9515295891e-4 * s + 8.3321608736e-3) * s - 1.6666654611e-1) * s * r + r
    cosine = ((2.443315711809948e-5 * s - 1.388731625493765e-3) * s + 4.166664568298827e-2) * (
        s * s
    ) + (1.0 - 0.5 * s)
    place = n - 4.0 * jnp.floor(n * 0.25)
    odd = (place == 1.0) | (place == 3.0)
    sin_sign = jnp.where(place >= 2.0, -1.0, 1.0)
    cos_sign = jnp.where((place == 1.0) | (place == 2.0), -1.0, 1.0)
    return sin_sign * jnp.where(odd, cosine, sine), cos_sign * jnp.where(odd, sine, cosine)


def split(x):
    high = x.astype(BF16)
    return high, (x - high.astype(F32)).astype(BF16)


def dot(a, b):
    return jnp.dot(a, b, preferred_element_type=F32)


def stacked(*parts):
    return split(jnp.concatenate(parts, axis=0))


def tall(a):
    return jnp.concatenate(a, axis=0)


def wide(b):
    return jnp.concatenate(b, axis=1)


def product(a, b):
    m, n = a.shape[0] // 2, b.shape[1] // 2
    c = dot(a, b)
    return c[:m, :n] + (c[:m, n:] + c[m:, :n])


def deep_left(a):
    high, low = split(a)
    return jnp.concatenate([high, low, high], axis=1)


def deep_right(b):
    high, low = split(b)
    return jnp.concatenate([high, high, low], axis=0)


def kernel(
    n_blk,
    n_box,
    points_hbm,
    angles_hbm,
    mask_hbm,
    skeleton_hbm,
    l_hbm,
    e_hbm,
    g_hbm,
    out_ref,
    points_ref,
    angles_ref,
    mask_ref,
    skeleton_ref,
    l_ref,
    e_ref,
    g_ref,
    u_ref,
    near_ref,
    mine_ref,
    t_ref,
    p_ref,
    above_ref,
    other_ref,
    x_ref,
    came_ref,
    load_sem,
    u_send,
    u_recv,
    t_send,
    t_recv,
    pair_send,
    pair_recv,
    w_send,
    w_recv,
    x_send,
    x_recv,
):
    r = lax.axis_index("blk")
    q = lax.axis_index("box")
    width = l_ref.shape[1]
    rank = u_ref.shape[1]
    count = u_ref.shape[2]
    share = count // n_box
    half = count // 2
    pairs = n_box // 2
    pair = q // 2
    side = lax.rem(q, 2)

    def around(dr, dq):
        return {"blk": lax.rem(r + dr + n_blk, n_blk), "box": lax.rem(q + dq + n_box, n_box)}

    def across(k):
        place = q
        bit = 1
        while bit <= k:
            if k & bit:
                place = place + bit - 2 * bit * lax.rem(q // bit, 2)
            bit *= 2
        return {"blk": r, "box": place}

    loads = [
        pltpu.make_async_copy(angles_hbm, angles_ref, load_sem.at[0]),
        pltpu.make_async_copy(points_hbm, points_ref, load_sem.at[1]),
        pltpu.make_async_copy(l_hbm.at[0], l_ref, load_sem.at[2]),
        pltpu.make_async_copy(e_hbm.at[0], e_ref, load_sem.at[3]),
        pltpu.make_async_copy(skeleton_hbm, skeleton_ref, load_sem.at[5]),
        pltpu.make_async_copy(mask_hbm, mask_ref, load_sem.at[6]),
        pltpu.make_async_copy(g_hbm.at[0], g_ref.at[0], load_sem.at[4]),
    ]
    for load in loads:
        load.start()

    barrier = pltpu.get_barrier_semaphore()
    greeted = [around(0, d) for d in range(1, n_box)]
    greeted += [around(dr, dq) for dr, dq in OFFSETS if dr != 0]
    for device in greeted:
        pl.semaphore_signal(barrier, inc=1, device_id=device, device_id_type=MESH)

    loads[0].wait()
    loads[1].wait()
    given = angles_ref[...].astype(F32)
    block = lax.broadcasted_iota(jnp.int32, (1, count), 1) // share
    theta = given
    for j in range(n_box):
        source = 2 * j if j < pairs else 2 * (j - pairs) + 1
        if source != j:
            moved = pltpu.roll(given, (j - source) % n_box * share, 1)
            theta = jnp.where(block == j, moved, theta)
    theta = theta * (2.0 * jnp.pi / SWEEP)
    sin_theta, cos_theta = sin_cos(theta)

    def column(i):
        return jnp.broadcast_to(points_ref[i : i + 1, :], (count, width)).T

    phase = WAVENUMBER * (
        column(0) * cos_theta + column(1) * (0.6 * sin_theta) + column(2) * (0.8 * sin_theta)
    )
    sine, cosine = sin_cos(phase)

    first = lax.broadcasted_iota(jnp.int32, (1, count), 1) < half

    def turned(a):
        return jnp.where(first, -1.0, 1.0) * pltpu.roll(a, half, 1)

    def complex_of(a):
        m = a.shape[0] // 2
        return a[:m] + turned(a[m:])

    def transposed_of(a):
        re, im = a[:, :width], a[:, width:]
        return jnp.stack([re[:half] - im[half:], re[half:] + im[:half]])

    field = [
        wide(split(jnp.where(first, cosine, pltpu.roll(sine, half, 1)))),
        wide(split(jnp.where(first, pltpu.roll(cosine, half, 1), sine))),
    ]

    loads[4].wait()
    row = lax.broadcasted_iota(jnp.int32, (rank, width), 0)
    lane = lax.broadcasted_iota(jnp.int32, (rank, width), 1)
    wanted = jnp.zeros((rank, width), jnp.int32)
    for k in range(rank):
        wanted = jnp.where(row == k, skeleton_ref[0, k], wanted)
    picker = jnp.where(wanted == lane, 1.0, 0.0).astype(BF16)

    def pick(a):
        return tuple(dot(picker, part).astype(BF16) for part in a)

    loads[2].wait()
    lr, li = split(l_ref[0]), split(l_ref[1])
    plr, pli = pick(lr), pick(li)
    picked = tall([plr[0], pli[0], plr[1], pli[1]])
    u = [complex_of(product(picked, part)) for part in field]
    for h in range(2):
        u_ref[h] = u[h]
    for i, part in enumerate((plr, pli)):
        p_ref[0, i] = part[0].astype(F32) + part[1].astype(F32)

    pl.semaphore_wait(barrier, len(greeted))

    u_copies = [[], []]
    for h in range(2):
        for m, (dr, dq) in enumerate(OFFSETS):
            copy = pltpu.make_async_remote_copy(
                src_ref=u_ref.at[h],
                dst_ref=near_ref.at[h, 7 - m],
                send_sem=u_send.at[h, m],
                recv_sem=u_recv.at[h, 7 - m],
                device_id=around(dr, dq),
                device_id_type=MESH,
            )
            copy.start()
            u_copies[h].append(copy)

    pair_copies = [
        pltpu.make_async_remote_copy(
            src_ref=ref.at[0],
            dst_ref=ref.at[1],
            send_sem=pair_send.at[i],
            recv_sem=pair_recv.at[i],
            device_id=across(1),
            device_id_type=MESH,
        )
        for i, ref in enumerate((g_ref, p_ref))
    ]
    loads[6].wait()
    for copy in pair_copies:
        copy.start()

    whole = tall([lr[0], li[0], lr[1], li[1]])
    z = [complex_of(product(whole, part)) for part in field]
    loads[3].wait()
    loads[5].wait()
    masked = [
        e_ref[m] * mask_ref[0, m].astype(F32) for m in range(len(OFFSETS))
    ]
    er = split(jnp.concatenate([e[0] for e in masked], axis=0).T)
    ei = split(jnp.concatenate([e[1] for e in masked], axis=0).T)
    per, pei = pick(er), pick(ei)
    coupling = tall([er[0], ei[0], er[1], ei[1]])
    picked_coupling = tall([per[0], pei[0], per[1], pei[1]])

    def send_t(h, d):
        return pltpu.make_async_remote_copy(
            src_ref=mine_ref.at[h],
            dst_ref=t_ref.at[q],
            send_sem=t_send.at[d],
            recv_sem=t_recv.at[d],
            device_id=across(d),
            device_id_type=MESH,
        )

    near = []
    for h in range(2):
        for copy in u_copies[h]:
            copy.wait_recv()
        near.append(wide(split(near_ref[h].reshape(len(OFFSETS) * rank, count))))
        mine_ref[h] = u[h] - complex_of(product(picked_coupling, near[h]))
        for d in sorted(range(1, n_box), key=lambda d: -d.bit_length()):

            @pl.when(lax.rem(q + d, 2) == h)
            def _(h=h, d=d):
                send_t(h, d).start()

    t_ref[pl.ds(q, 1)] = mine_ref[pl.ds(side, 1)]

    below = deep_right(jnp.concatenate([l_ref[0], l_ref[1]], axis=1))
    for h in range(2):
        w = z[h] - complex_of(product(coupling, near[h]))
        above_ref[h] = transposed_of(dot(deep_left(w.T), below))

    def send_w(to):
        return pltpu.make_async_remote_copy(
            src_ref=above_ref.at[1 - side, :, pl.ds(to * share, share)],
            dst_ref=other_ref.at[pair],
            send_sem=w_send.at[to],
            recv_sem=w_recv.at[pair],
            device_id={"blk": r, "box": 2 * to + 1 - side},
            device_id_type=MESH,
        )

    for to in range(pairs):
        send_w(to).start()

    for copy in pair_copies:
        copy.wait_recv()
    top = tall(stacked(g_ref[0, 0], g_ref[1, 0], g_ref[0, 1], g_ref[1, 1]))
    none = jnp.zeros((rank, width), F32)
    spread = deep_right(
        jnp.concatenate(
            [
                jnp.concatenate([p_ref[0, 0], p_ref[0, 1], none, none], axis=1),
                jnp.concatenate([none, none, p_ref[1, 0], p_ref[1, 1]], axis=1),
            ],
            axis=0,
        )
    )

    for d in range(1, n_box):
        send_t(0, d).wait_recv()
    y = complex_of(product(top, wide(split(t_ref[...].reshape(n_box * rank, count)))))
    x = dot(deep_left(y.T), spread)
    x_ref[0] = above_ref[side] + transposed_of(x[:, : 2 * width])
    x_ref[1] = transposed_of(x[:, 2 * width :])

    def send_x(to, here):
        return pltpu.make_async_remote_copy(
            src_ref=x_ref.at[:, :, pl.ds(to * share, share)],
            dst_ref=came_ref.at[here],
            send_sem=x_send.at[to],
            recv_sem=x_recv.at[here],
            device_id={"blk": r, "box": 2 * to + side},
            device_id_type=MESH,
        )

    for to in range(pairs):

        @pl.when(pair != to)
        def _(to=to):
            send_x(to, pair).start()

    def place(box):
        return pl.ds(pl.multiple_of(box * width, width), width)

    for here in range(pairs):
        pltpu.make_async_remote_copy(
            src_ref=above_ref.at[0, :, pl.ds(0, share)],
            dst_ref=other_ref.at[here],
            send_sem=w_send.at[here],
            recv_sem=w_recv.at[here],
            device_id=across(1),
            device_id_type=MESH,
        ).wait_recv()

    own = pl.ds(pl.multiple_of(pair * share, share), share)
    out_ref[:, :, place(q)] = x_ref[0, :, own]
    out_ref[:, :, place(2 * pair + 1 - side)] = x_ref[1, :, own] + other_ref[pair]

    for here in range(pairs):

        @pl.when(pair != here)
        def _(here=here):
            send_x(here, here).wait_recv()
            out_ref[:, :, place(2 * here + side)] = came_ref[here, 0]
            out_ref[:, :, place(2 * here + 1 - side)] = came_ref[here, 1] + other_ref[here]

    for copy in u_copies[0] + u_copies[1] + pair_copies:
        copy.wait_send()
    for d in range(1, n_box):
        send_t(0, d).wait_send()
    for to in range(pairs):
        send_w(to).wait_send()

        @pl.when(pair != to)
        def _(to=to):
            send_x(to, pair).wait_send()


def on_device(
    n_blk,
    n_box,
    surface_points,
    angle_ids,
    near_mask,
    skeleton,
    box_inverse_parts,
    near_coupling,
    top_inverse,
):
    width = box_inverse_parts.shape[2]
    count = angle_ids.shape[0]
    rank = skeleton.shape[1]
    vmem = pl.BlockSpec(memory_space=pltpu.VMEM)
    hbm = pl.BlockSpec(memory_space=pl.ANY)
    return pl.pallas_call(
        functools.partial(kernel, n_blk, n_box),
        out_shape=jax.ShapeDtypeStruct((2, count // n_box, n_box * width), F32),
        in_specs=[hbm] * 7,
        out_specs=vmem,
        scratch_shapes=[
            pltpu.VMEM(surface_points.shape, F32),
            pltpu.VMEM((1, count), jnp.int32),
            pltpu.SMEM(near_mask.shape, jnp.int32),
            pltpu.SMEM(skeleton.shape, jnp.int32),
            pltpu.VMEM(box_inverse_parts.shape[1:], F32),
            pltpu.VMEM(near_coupling.shape[1:], F32),
            pltpu.VMEM((2, *top_inverse.shape[1:]), F32),
            pltpu.VMEM((2, rank, count), F32),
            pltpu.VMEM((2, len(OFFSETS), rank, count), F32),
            pltpu.VMEM((2, rank, count), F32),
            pltpu.VMEM((n_box, rank, count), F32),
            pltpu.VMEM((2, 2, rank, width), F32),
            pltpu.VMEM((2, 2, count // 2, width), F32),
            pltpu.VMEM((n_box // 2, 2, count // n_box, width), F32),
            pltpu.VMEM((2, 2, count // 2, width), F32),
            pltpu.VMEM((n_box // 2, 2, 2, count // n_box, width), F32),
            pltpu.SemaphoreType.DMA((7,)),
            pltpu.SemaphoreType.DMA((2, len(OFFSETS))),
            pltpu.SemaphoreType.DMA((2, len(OFFSETS))),
            pltpu.SemaphoreType.DMA((n_box,)),
            pltpu.SemaphoreType.DMA((n_box,)),
            pltpu.SemaphoreType.DMA((2,)),
            pltpu.SemaphoreType.DMA((2,)),
            pltpu.SemaphoreType.DMA((n_box // 2,)),
            pltpu.SemaphoreType.DMA((n_box // 2,)),
            pltpu.SemaphoreType.DMA((n_box // 2,)),
            pltpu.SemaphoreType.DMA((n_box // 2,)),
        ],
        compiler_params=pltpu.CompilerParams(
            collective_id=0, has_side_effects=True, vmem_limit_bytes=16 * 1024 * 1024
        ),
    )(
        *(
            pltpu.with_memory_space_constraint(a, pltpu.HBM)
            for a in (
                surface_points,
                angle_ids.reshape(1, count),
                near_mask,
                skeleton,
                box_inverse_parts,
                near_coupling,
                top_inverse,
            )
        )
    )


def solution(mesh):
    return jax.shard_map(
        functools.partial(on_device, mesh.shape["blk"], mesh.shape["box"]),
        mesh=mesh,
        in_specs=(
            P(None, ("blk", "box")),
            P("batch"),
            P(("blk", "box"), None),
            P(("blk", "box"), None),
            P(("blk", "box"), None, None, None),
            P(("blk", "box"), None, None, None, None),
            P("blk", None, "box", None),
        ),
        out_specs=P(None, ("batch", "box"), "blk"),
        check_vma=False,
    )
```

```python
import functools

import jax
import jax.numpy as jnp
from jax import lax
from jax.experimental import pallas as pl
from jax.experimental.pallas import tpu as pltpu
from jax.sharding import PartitionSpec as P

SWEEP = 16384
WAVENUMBER = 24.0
OFFSETS = ((-1, -1), (-1, 0), (-1, 1), (0, -1), (0, 1), (1, -1), (1, 0), (1, 1))
MESH = pl.DeviceIdType.MESH
F32 = jnp.float32
BF16 = jnp.bfloat16


def sin_cos(x):
    n = jnp.round(x * (2.0 / jnp.pi))
    r = x - n * 1.5703125
    r = r - n * 4.8375129699707031e-4
    r = r - n * 7.5497899548918822e-8
    s = r * r
    sine = ((-1.9515295891e-4 * s + 8.3321608736e-3) * s - 1.6666654611e-1) * s * r + r
    cosine = ((2.443315711809948e-5 * s - 1.388731625493765e-3) * s + 4.166664568298827e-2) * (
        s * s
    ) + (1.0 - 0.5 * s)
    place = n - 4.0 * jnp.floor(n * 0.25)
    odd = (place == 1.0) | (place == 3.0)
    sin_sign = jnp.where(place >= 2.0, -1.0, 1.0)
    cos_sign = jnp.where((place == 1.0) | (place == 2.0), -1.0, 1.0)
    return sin_sign * jnp.where(odd, cosine, sine), cos_sign * jnp.where(odd, sine, cosine)


def split(x):
    high = x.astype(BF16)
    return high, (x - high.astype(F32)).astype(BF16)


def dot(a, b):
    return jnp.dot(a, b, preferred_element_type=F32)


def stacked(*parts):
    return split(jnp.concatenate(parts, axis=0))


def tall(a):
    return jnp.concatenate(a, axis=0)


def wide(b):
    return jnp.concatenate(b, axis=1)


def product(a, b):
    m, n = a.shape[0] // 2, b.shape[1] // 2
    c = dot(a, b)
    return c[:m, :n] + (c[:m, n:] + c[m:, :n])


def deep_left(a):
    high, low = split(a)
    return jnp.concatenate([high, low, high], axis=1)


def deep_right(b):
    high, low = split(b)
    return jnp.concatenate([high, high, low], axis=0)


def kernel(
    n_blk,
    n_box,
    points_hbm,
    angles_hbm,
    mask_hbm,
    skeleton_hbm,
    l_hbm,
    e_hbm,
    g_hbm,
    out_ref,
    points_ref,
    angles_ref,
    mask_ref,
    skeleton_ref,
    l_ref,
    e_ref,
    g_ref,
    u_ref,
    near_ref,
    mine_ref,
    t_ref,
    p_ref,
    above_ref,
    other_ref,
    x_ref,
    came_ref,
    held_ref,
    load_sem,
    u_send,
    u_recv,
    t_send,
    t_recv,
    pair_send,
    pair_recv,
    own_send,
    own_recv,
    w_send,
    w_recv,
    x_send,
    x_recv,
):
    r = lax.axis_index("blk")
    q = lax.axis_index("box")
    width = l_ref.shape[1]
    rank = u_ref.shape[1]
    count = u_ref.shape[2]
    share = count // n_box
    half = count // 2
    pairs = n_box // 2
    pair = q // 2
    side = lax.rem(q, 2)
    mate = r + 1 - 2 * lax.rem(r, 2)
    beyond = lax.rem(r - 1 + 2 * lax.rem(r, 2) + n_blk, n_blk)

    def around(dr, dq):
        return {"blk": lax.rem(r + dr + n_blk, n_blk), "box": lax.rem(q + dq + n_box, n_box)}

    def across(k):
        place = q
        bit = 1
        while bit <= k:
            if k & bit:
                place = place + bit - 2 * bit * lax.rem(q // bit, 2)
            bit *= 2
        return {"blk": mate, "box": place}

    loads = [
        pltpu.make_async_copy(angles_hbm, angles_ref, load_sem.at[0]),
        pltpu.make_async_copy(points_hbm, points_ref, load_sem.at[1]),
        pltpu.make_async_copy(l_hbm.at[0], l_ref, load_sem.at[2]),
        pltpu.make_async_copy(e_hbm.at[0], e_ref, load_sem.at[3]),
        pltpu.make_async_copy(skeleton_hbm, skeleton_ref, load_sem.at[5]),
        pltpu.make_async_copy(mask_hbm, mask_ref, load_sem.at[6]),
        pltpu.make_async_copy(g_hbm.at[0], g_ref.at[0], load_sem.at[4]),
    ]
    for load in loads:
        load.start()

    barrier = pltpu.get_barrier_semaphore()
    greeted = [around(0, d) for d in range(1, n_box)]
    greeted += [{"blk": mate, "box": to} for to in range(n_box)]
    greeted += [{"blk": beyond, "box": around(0, dq)["box"]} for dq in (-1, 0, 1)]
    for device in greeted:
        pl.semaphore_signal(barrier, inc=1, device_id=device, device_id_type=MESH)

    loads[0].wait()
    loads[1].wait()
    given = angles_ref[...].astype(F32)
    block = lax.broadcasted_iota(jnp.int32, (1, count), 1) // share
    theta = given
    for j in range(n_box):
        source = 2 * j if j < pairs else 2 * (j - pairs) + 1
        if source != j:
            moved = pltpu.roll(given, (j - source) % n_box * share, 1)
            theta = jnp.where(block == j, moved, theta)
    theta = theta * (2.0 * jnp.pi / SWEEP)
    sin_theta, cos_theta = sin_cos(theta)

    def column(i):
        return jnp.broadcast_to(points_ref[i : i + 1, :], (count, width)).T

    phase = WAVENUMBER * (
        column(0) * cos_theta + column(1) * (0.6 * sin_theta) + column(2) * (0.8 * sin_theta)
    )
    sine, cosine = sin_cos(phase)

    first = lax.broadcasted_iota(jnp.int32, (1, count), 1) < half

    def turned(a):
        return jnp.where(first, -1.0, 1.0) * pltpu.roll(a, half, 1)

    def complex_of(a):
        m = a.shape[0] // 2
        return a[:m] + turned(a[m:])

    def transposed_of(a):
        re, im = a[:, :width], a[:, width:]
        return jnp.stack([re[:half] - im[half:], re[half:] + im[:half]])

    field = [
        wide(split(jnp.where(first, cosine, pltpu.roll(sine, half, 1)))),
        wide(split(jnp.where(first, pltpu.roll(cosine, half, 1), sine))),
    ]

    loads[4].wait()
    row = lax.broadcasted_iota(jnp.int32, (rank, width), 0)
    lane = lax.broadcasted_iota(jnp.int32, (rank, width), 1)
    wanted = jnp.zeros((rank, width), jnp.int32)
    for k in range(rank):
        wanted = jnp.where(row == k, skeleton_ref[0, k], wanted)
    picker = jnp.where(wanted == lane, 1.0, 0.0).astype(BF16)

    def pick(a):
        return tuple(dot(picker, part).astype(BF16) for part in a)

    loads[2].wait()
    lr, li = split(l_ref[0]), split(l_ref[1])
    plr, pli = pick(lr), pick(li)
    picked = tall([plr[0], pli[0], plr[1], pli[1]])
    u = [complex_of(product(picked, part)) for part in field]
    for h in range(2):
        u_ref[h] = u[h]
    for i, part in enumerate((plr, pli)):
        p_ref[0, i] = part[0].astype(F32) + part[1].astype(F32)

    pl.semaphore_wait(barrier, len(greeted))

    u_copies = [[], []]
    for h in range(2):
        for m, (dr, dq) in enumerate(OFFSETS):
            copy = pltpu.make_async_remote_copy(
                src_ref=u_ref.at[h],
                dst_ref=near_ref.at[h, 7 - m],
                send_sem=u_send.at[h, m],
                recv_sem=u_recv.at[h, 7 - m],
                device_id=around(dr, dq),
                device_id_type=MESH,
            )
            copy.start()
            u_copies[h].append(copy)

    pair_copies = [
        pltpu.make_async_remote_copy(
            src_ref=ref.at[0],
            dst_ref=ref.at[1 + d],
            send_sem=pair_send.at[i, d],
            recv_sem=pair_recv.at[i, d],
            device_id=across(d),
            device_id_type=MESH,
        )
        for d in (1, 0)
        for i, ref in enumerate((g_ref, p_ref))
    ]
    loads[6].wait()
    for copy in pair_copies:
        copy.start()

    whole = tall([lr[0], li[0], lr[1], li[1]])
    z = [complex_of(product(whole, part)) for part in field]
    loads[3].wait()
    loads[5].wait()
    masked = [
        e_ref[m] * mask_ref[0, m].astype(F32) for m in range(len(OFFSETS))
    ]
    er = split(jnp.concatenate([e[0] for e in masked], axis=0).T)
    ei = split(jnp.concatenate([e[1] for e in masked], axis=0).T)
    per, pei = pick(er), pick(ei)
    coupling = tall([er[0], ei[0], er[1], ei[1]])
    picked_coupling = tall([per[0], pei[0], per[1], pei[1]])

    def send_t(h, d):
        return pltpu.make_async_remote_copy(
            src_ref=mine_ref.at[h],
            dst_ref=t_ref.at[q],
            send_sem=t_send.at[d],
            recv_sem=t_recv.at[d],
            device_id=across(d),
            device_id_type=MESH,
        )

    near = []
    for h in range(2):
        for copy in u_copies[h]:
            copy.wait_recv()
        near.append(wide(split(near_ref[h].reshape(len(OFFSETS) * rank, count))))
        mine_ref[h] = u[h] - complex_of(product(picked_coupling, near[h]))
        for d in sorted(range(n_box), key=lambda d: -d.bit_length()):

            @pl.when(lax.rem(q + d, 2) == h)
            def _(h=h, d=d):
                send_t(h, d).start()

    below = deep_right(jnp.concatenate([l_ref[0], l_ref[1]], axis=1))
    for h in range(2):
        w = z[h] - complex_of(product(coupling, near[h]))
        above_ref[h] = transposed_of(dot(deep_left(w.T), below))

    def send_w(to):
        return pltpu.make_async_remote_copy(
            src_ref=above_ref.at[1 - side, :, pl.ds(to * share, share)],
            dst_ref=other_ref.at[pair],
            send_sem=w_send.at[to],
            recv_sem=w_recv.at[pair],
            device_id={"blk": r, "box": 2 * to + 1 - side},
            device_id_type=MESH,
        )

    own_half = pltpu.make_async_remote_copy(
        src_ref=above_ref.at[side],
        dst_ref=held_ref,
        send_sem=own_send,
        recv_sem=own_recv,
        device_id=across(0),
        device_id_type=MESH,
    )
    own_half.start()
    for to in range(pairs):
        send_w(to).start()

    for copy in pair_copies:
        copy.wait_recv()
    top = tall(stacked(g_ref[1, 0], g_ref[2, 0], g_ref[1, 1], g_ref[2, 1]))
    none = jnp.zeros((rank, width), F32)
    spread = deep_right(
        jnp.concatenate(
            [
                jnp.concatenate([p_ref[1, 0], p_ref[1, 1], none, none], axis=1),
                jnp.concatenate([none, none, p_ref[2, 0], p_ref[2, 1]], axis=1),
            ],
            axis=0,
        )
    )

    own_half.wait_recv()
    for d in range(n_box):
        send_t(0, d).wait_recv()
    y = complex_of(product(top, wide(split(t_ref[...].reshape(n_box * rank, count)))))
    x = dot(deep_left(y.T), spread)
    x_ref[0] = held_ref[...] + transposed_of(x[:, : 2 * width])
    x_ref[1] = transposed_of(x[:, 2 * width :])

    def send_x(to, here):
        return pltpu.make_async_remote_copy(
            src_ref=x_ref.at[:, :, pl.ds(to * share, share)],
            dst_ref=came_ref.at[here],
            send_sem=x_send.at[to],
            recv_sem=x_recv.at[here],
            device_id={"blk": mate, "box": 2 * to + side},
            device_id_type=MESH,
        )

    for to in range(pairs):
        send_x(to, pair).start()

    def place(box):
        return pl.ds(pl.multiple_of(box * width, width), width)

    for here in range(pairs):
        pltpu.make_async_remote_copy(
            src_ref=above_ref.at[0, :, pl.ds(0, share)],
            dst_ref=other_ref.at[here],
            send_sem=w_send.at[here],
            recv_sem=w_recv.at[here],
            device_id=across(1),
            device_id_type=MESH,
        ).wait_recv()

    for here in range(pairs):
        send_x(here, here).wait_recv()
        out_ref[:, :, place(2 * here + side)] = came_ref[here, 0]
        out_ref[:, :, place(2 * here + 1 - side)] = came_ref[here, 1] + other_ref[here]

    for copy in u_copies[0] + u_copies[1] + pair_copies:
        copy.wait_send()
    own_half.wait_send()
    for d in range(n_box):
        send_t(0, d).wait_send()
    for to in range(pairs):
        send_w(to).wait_send()
        send_x(to, pair).wait_send()


def on_device(
    n_blk,
    n_box,
    surface_points,
    angle_ids,
    near_mask,
    skeleton,
    box_inverse_parts,
    near_coupling,
    top_inverse,
):
    width = box_inverse_parts.shape[2]
    count = angle_ids.shape[0]
    rank = skeleton.shape[1]
    vmem = pl.BlockSpec(memory_space=pltpu.VMEM)
    hbm = pl.BlockSpec(memory_space=pl.ANY)
    return pl.pallas_call(
        functools.partial(kernel, n_blk, n_box),
        out_shape=jax.ShapeDtypeStruct((2, count // n_box, n_box * width), F32),
        in_specs=[hbm] * 7,
        out_specs=vmem,
        scratch_shapes=[
            pltpu.VMEM(surface_points.shape, F32),
            pltpu.VMEM((1, count), jnp.int32),
            pltpu.SMEM(near_mask.shape, jnp.int32),
            pltpu.SMEM(skeleton.shape, jnp.int32),
            pltpu.VMEM(box_inverse_parts.shape[1:], F32),
            pltpu.VMEM(near_coupling.shape[1:], F32),
            pltpu.VMEM((3, *top_inverse.shape[1:]), F32),
            pltpu.VMEM((2, rank, count), F32),
            pltpu.VMEM((2, len(OFFSETS), rank, count), F32),
            pltpu.VMEM((2, rank, count), F32),
            pltpu.VMEM((n_box, rank, count), F32),
            pltpu.VMEM((3, 2, rank, width), F32),
            pltpu.VMEM((2, 2, count // 2, width), F32),
            pltpu.VMEM((n_box // 2, 2, count // n_box, width), F32),
            pltpu.VMEM((2, 2, count // 2, width), F32),
            pltpu.VMEM((n_box // 2, 2, 2, count // n_box, width), F32),
            pltpu.VMEM((2, count // 2, width), F32),
            pltpu.SemaphoreType.DMA((7,)),
            pltpu.SemaphoreType.DMA((2, len(OFFSETS))),
            pltpu.SemaphoreType.DMA((2, len(OFFSETS))),
            pltpu.SemaphoreType.DMA((n_box,)),
            pltpu.SemaphoreType.DMA((n_box,)),
            pltpu.SemaphoreType.DMA((2, 2)),
            pltpu.SemaphoreType.DMA((2, 2)),
            pltpu.SemaphoreType.DMA,
            pltpu.SemaphoreType.DMA,
            pltpu.SemaphoreType.DMA((n_box // 2,)),
            pltpu.SemaphoreType.DMA((n_box // 2,)),
            pltpu.SemaphoreType.DMA((n_box // 2,)),
            pltpu.SemaphoreType.DMA((n_box // 2,)),
        ],
        compiler_params=pltpu.CompilerParams(
            collective_id=0, has_side_effects=True, vmem_limit_bytes=16 * 1024 * 1024
        ),
    )(
        *(
            pltpu.with_memory_space_constraint(a, pltpu.HBM)
            for a in (
                surface_points,
                angle_ids.reshape(1, count),
                near_mask,
                skeleton,
                box_inverse_parts,
                near_coupling,
                top_inverse,
            )
        )
    )


def solution(mesh):
    return jax.shard_map(
        functools.partial(on_device, mesh.shape["blk"], mesh.shape["box"]),
        mesh=mesh,
        in_specs=(
            P(None, ("blk", "box")),
            P("batch"),
            P(("blk", "box"), None),
            P(("blk", "box"), None),
            P(("blk", "box"), None, None, None),
            P(("blk", "box"), None, None, None, None),
            P("blk", None, "box", None),
        ),
        out_specs=P(None, ("batch", "box"), "blk"),
        check_vma=False,
    )
```

```python
import functools

import jax
import jax.numpy as jnp
from jax import lax
from jax.experimental import pallas as pl
from jax.experimental.pallas import tpu as pltpu
from jax.sharding import PartitionSpec as P

SWEEP = 16384
WAVENUMBER = 24.0
OFFSETS = ((-1, -1), (-1, 0), (-1, 1), (0, -1), (0, 1), (1, -1), (1, 0), (1, 1))
MESH = pl.DeviceIdType.MESH
F32 = jnp.float32
BF16 = jnp.bfloat16


def sin_cos(x):
    n = jnp.round(x * (2.0 / jnp.pi))
    r = x - n * 1.5703125
    r = r - n * 4.8375129699707031e-4
    r = r - n * 7.5497899548918822e-8
    s = r * r
    sine = ((-1.9515295891e-4 * s + 8.3321608736e-3) * s - 1.6666654611e-1) * s * r + r
    cosine = ((2.443315711809948e-5 * s - 1.388731625493765e-3) * s + 4.166664568298827e-2) * (
        s * s
    ) + (1.0 - 0.5 * s)
    place = n - 4.0 * jnp.floor(n * 0.25)
    odd = (place == 1.0) | (place == 3.0)
    sin_sign = jnp.where(place >= 2.0, -1.0, 1.0)
    cos_sign = jnp.where((place == 1.0) | (place == 2.0), -1.0, 1.0)
    return sin_sign * jnp.where(odd, cosine, sine), cos_sign * jnp.where(odd, sine, cosine)


def split(x):
    high = x.astype(BF16)
    return high, (x - high.astype(F32)).astype(BF16)


def dot(a, b):
    return jnp.dot(a, b, preferred_element_type=F32)


def tall(a):
    return jnp.concatenate(a, axis=0)


def wide(b):
    return jnp.concatenate(b, axis=1)


def product(a, b):
    m, n = a.shape[0] // 2, b.shape[1] // 2
    c = dot(a, b)
    return c[:m, :n] + (c[:m, n:] + c[m:, :n])


def deep_left(a):
    high, low = split(a)
    return jnp.concatenate([high, low, high], axis=1)


def deep_right(b):
    high, low = split(b)
    return jnp.concatenate([high, high, low], axis=0)


def kernel(
    n_blk,
    n_box,
    points_hbm,
    angles_hbm,
    mask_hbm,
    skeleton_hbm,
    l_hbm,
    e_hbm,
    g_hbm,
    out_ref,
    points_ref,
    angles_ref,
    mask_ref,
    skeleton_ref,
    l_ref,
    e_ref,
    g_ref,
    u_ref,
    near_ref,
    mine_ref,
    t_ref,
    p_ref,
    above_ref,
    other_ref,
    x_ref,
    came_ref,
    held_ref,
    joined_ref,
    load_sem,
    u_send,
    u_recv,
    t_send,
    t_recv,
    pair_send,
    pair_recv,
    own_send,
    own_recv,
    w_send,
    w_recv,
    x_send,
    x_recv,
):
    r = lax.axis_index("blk")
    q = lax.axis_index("box")
    width = l_ref.shape[1]
    rank = u_ref.shape[1]
    count = u_ref.shape[2]
    share = count // n_box
    half = count // 2
    pairs = n_box // 2
    pair = q // 2
    side = lax.rem(q, 2)
    mate = r + 1 - 2 * lax.rem(r, 2)
    beyond = lax.rem(r - 1 + 2 * lax.rem(r, 2) + n_blk, n_blk)

    def around(dr, dq):
        return {"blk": lax.rem(r + dr + n_blk, n_blk), "box": lax.rem(q + dq + n_box, n_box)}

    def across(k):
        place = q
        bit = 1
        while bit <= k:
            if k & bit:
                place = place + bit - 2 * bit * lax.rem(q // bit, 2)
            bit *= 2
        return {"blk": mate, "box": place}

    loads = [
        pltpu.make_async_copy(angles_hbm, angles_ref, load_sem.at[0]),
        pltpu.make_async_copy(points_hbm, points_ref, load_sem.at[1]),
        pltpu.make_async_copy(l_hbm.at[0], l_ref, load_sem.at[2]),
        pltpu.make_async_copy(e_hbm.at[0], e_ref, load_sem.at[3]),
        pltpu.make_async_copy(skeleton_hbm, skeleton_ref, load_sem.at[5]),
        pltpu.make_async_copy(mask_hbm, mask_ref, load_sem.at[6]),
        pltpu.make_async_copy(g_hbm.at[0], g_ref.at[0], load_sem.at[4]),
    ]
    for load in loads:
        load.start()

    barrier = pltpu.get_barrier_semaphore()
    greeted = [around(0, d) for d in range(1, n_box)]
    greeted += [{"blk": mate, "box": to} for to in range(n_box)]
    greeted += [{"blk": beyond, "box": around(0, dq)["box"]} for dq in (-1, 0, 1)]
    for device in greeted:
        pl.semaphore_signal(barrier, inc=1, device_id=device, device_id_type=MESH)

    loads[0].wait()
    loads[1].wait()
    given = angles_ref[...].astype(F32)
    block = lax.broadcasted_iota(jnp.int32, (1, count), 1) // share
    theta = given
    for j in range(n_box):
        source = 2 * j if j < pairs else 2 * (j - pairs) + 1
        if source != j:
            moved = pltpu.roll(given, (j - source) % n_box * share, 1)
            theta = jnp.where(block == j, moved, theta)
    theta = theta * (2.0 * jnp.pi / SWEEP)
    sin_theta, cos_theta = sin_cos(theta)

    def column(i):
        return jnp.broadcast_to(points_ref[i : i + 1, :], (count, width)).T

    phase = WAVENUMBER * (
        column(0) * cos_theta + column(1) * (0.6 * sin_theta) + column(2) * (0.8 * sin_theta)
    )
    sine, cosine = sin_cos(phase)

    first = lax.broadcasted_iota(jnp.int32, (1, count), 1) < half

    def turned(a):
        return jnp.where(first, -1.0, 1.0) * pltpu.roll(a, half, 1)

    def complex_of(a):
        m = a.shape[0] // 2
        return a[:m] + turned(a[m:])

    def transposed_of(a):
        re, im = a[:, :width], a[:, width:]
        return jnp.stack([re[:half] - im[half:], re[half:] + im[:half]])

    field = [
        wide(split(jnp.where(first, cosine, pltpu.roll(sine, half, 1)))),
        wide(split(jnp.where(first, pltpu.roll(cosine, half, 1), sine))),
    ]

    loads[4].wait()
    row = lax.broadcasted_iota(jnp.int32, (rank, width), 0)
    lane = lax.broadcasted_iota(jnp.int32, (rank, width), 1)
    wanted = jnp.zeros((rank, width), jnp.int32)
    for k in range(rank):
        wanted = jnp.where(row == k, skeleton_ref[0, k], wanted)
    picker = jnp.where(wanted == lane, 1.0, 0.0).astype(BF16)

    def pick(a):
        return tuple(dot(picker, part).astype(BF16) for part in a)

    loads[2].wait()
    lr, li = split(l_ref[0]), split(l_ref[1])
    plr, pli = pick(lr), pick(li)
    picked = tall([plr[0], pli[0], plr[1], pli[1]])
    u = [complex_of(product(picked, part)) for part in field]
    for h in range(2):
        u_ref[h] = u[h]
    for i, part in enumerate((plr, pli)):
        p_ref[0, i] = part[0].astype(F32) + part[1].astype(F32)

    pl.semaphore_wait(barrier, len(greeted))

    u_copies = [[], []]
    for h in range(2):
        for m, (dr, dq) in enumerate(OFFSETS):
            copy = pltpu.make_async_remote_copy(
                src_ref=u_ref.at[h],
                dst_ref=near_ref.at[h, 7 - m],
                send_sem=u_send.at[h, m],
                recv_sem=u_recv.at[h, 7 - m],
                device_id=around(dr, dq),
                device_id_type=MESH,
            )
            copy.start()
            u_copies[h].append(copy)

    pair_copies = [
        pltpu.make_async_remote_copy(
            src_ref=ref.at[0],
            dst_ref=ref.at[1 + d],
            send_sem=pair_send.at[i, d],
            recv_sem=pair_recv.at[i, d],
            device_id=across(d),
            device_id_type=MESH,
        )
        for d in (1, 0)
        for i, ref in enumerate((g_ref, p_ref))
    ]
    loads[6].wait()
    for copy in pair_copies:
        copy.start()

    whole = tall([lr[0], li[0], lr[1], li[1]])
    z = [complex_of(product(whole, part)) for part in field]
    loads[3].wait()
    loads[5].wait()
    masked = [
        e_ref[m] * mask_ref[0, m].astype(F32) for m in range(len(OFFSETS))
    ]
    er = split(jnp.concatenate([e[0] for e in masked], axis=0).T)
    ei = split(jnp.concatenate([e[1] for e in masked], axis=0).T)
    per, pei = pick(er), pick(ei)
    coupling = tall([er[0], ei[0], er[1], ei[1]])
    picked_coupling = tall([per[0], pei[0], per[1], pei[1]])

    def send_t(h, d):
        return pltpu.make_async_remote_copy(
            src_ref=mine_ref.at[h],
            dst_ref=t_ref.at[q],
            send_sem=t_send.at[d],
            recv_sem=t_recv.at[d],
            device_id=across(d),
            device_id_type=MESH,
        )

    near = []
    for h in range(2):
        for copy in u_copies[h]:
            copy.wait_recv()
        near.append(wide(split(near_ref[h].reshape(len(OFFSETS) * rank, count))))
        mine_ref[h] = u[h] - complex_of(product(picked_coupling, near[h]))
        for d in sorted(range(n_box), key=lambda d: -d.bit_length()):

            @pl.when(lax.rem(q + d, 2) == h)
            def _(h=h, d=d):
                send_t(h, d).start()

    below = deep_right(jnp.concatenate([l_ref[0], l_ref[1]], axis=1))
    for h in range(2):
        w = z[h] - complex_of(product(coupling, near[h]))
        above_ref[h] = transposed_of(dot(deep_left(w.T), below))

    def send_w(to):
        return pltpu.make_async_remote_copy(
            src_ref=above_ref.at[1 - side, :, pl.ds(to * share, share)],
            dst_ref=other_ref.at[pair],
            send_sem=w_send.at[to],
            recv_sem=w_recv.at[pair],
            device_id={"blk": r, "box": 2 * to + 1 - side},
            device_id_type=MESH,
        )

    own_half = pltpu.make_async_remote_copy(
        src_ref=above_ref.at[side],
        dst_ref=held_ref,
        send_sem=own_send,
        recv_sem=own_recv,
        device_id=across(0),
        device_id_type=MESH,
    )
    own_half.start()
    for to in range(pairs):
        send_w(to).start()

    for copy in pair_copies:
        copy.wait_recv()
    joined = jnp.concatenate(
        [
            dot(
                deep_left(jnp.concatenate([g_ref[i, 0], g_ref[i, 1]], axis=0).T),
                deep_right(
                    jnp.concatenate(
                        [
                            jnp.concatenate([p_ref[i, 0], p_ref[i, 1]], axis=1),
                            jnp.concatenate([-p_ref[i, 1], p_ref[i, 0]], axis=1),
                        ],
                        axis=0,
                    )
                ),
            )
            for i in (1, 2)
        ],
        axis=1,
    )
    depth = pairs * rank
    for g in range(2):
        joined_ref[g] = deep_right(joined[g * depth : (g + 1) * depth])

    def part_of_x(g):
        t = t_ref[pl.ds(g * pairs, pairs)].reshape(depth, count)
        return dot(deep_left(t.T), joined_ref[g])

    near_half = q // pairs
    for d in range(pairs):
        send_t(0, d).wait_recv()
    x = part_of_x(near_half)
    own_half.wait_recv()
    for d in range(pairs, n_box):
        send_t(0, d).wait_recv()
    x = x + part_of_x(1 - near_half)
    x_ref[0] = held_ref[...] + transposed_of(x[:, : 2 * width])
    x_ref[1] = transposed_of(x[:, 2 * width :])

    def send_x(to, here):
        return pltpu.make_async_remote_copy(
            src_ref=x_ref.at[:, :, pl.ds(to * share, share)],
            dst_ref=came_ref.at[here],
            send_sem=x_send.at[to],
            recv_sem=x_recv.at[here],
            device_id={"blk": mate, "box": 2 * to + side},
            device_id_type=MESH,
        )

    for to in range(pairs):
        send_x(to, pair).start()

    def place(box):
        return pl.ds(pl.multiple_of(box * width, width), width)

    for here in range(pairs):
        pltpu.make_async_remote_copy(
            src_ref=above_ref.at[0, :, pl.ds(0, share)],
            dst_ref=other_ref.at[here],
            send_sem=w_send.at[here],
            recv_sem=w_recv.at[here],
            device_id=across(1),
            device_id_type=MESH,
        ).wait_recv()

    for here in range(pairs):
        send_x(here, here).wait_recv()
        out_ref[:, :, place(2 * here + side)] = came_ref[here, 0]
        out_ref[:, :, place(2 * here + 1 - side)] = came_ref[here, 1] + other_ref[here]

    for copy in u_copies[0] + u_copies[1] + pair_copies:
        copy.wait_send()
    own_half.wait_send()
    for d in range(n_box):
        send_t(0, d).wait_send()
    for to in range(pairs):
        send_w(to).wait_send()
        send_x(to, pair).wait_send()


def on_device(
    n_blk,
    n_box,
    surface_points,
    angle_ids,
    near_mask,
    skeleton,
    box_inverse_parts,
    near_coupling,
    top_inverse,
):
    width = box_inverse_parts.shape[2]
    count = angle_ids.shape[0]
    rank = skeleton.shape[1]
    vmem = pl.BlockSpec(memory_space=pltpu.VMEM)
    hbm = pl.BlockSpec(memory_space=pl.ANY)
    return pl.pallas_call(
        functools.partial(kernel, n_blk, n_box),
        out_shape=jax.ShapeDtypeStruct((2, count // n_box, n_box * width), F32),
        in_specs=[hbm] * 7,
        out_specs=vmem,
        scratch_shapes=[
            pltpu.VMEM(surface_points.shape, F32),
            pltpu.VMEM((1, count), jnp.int32),
            pltpu.SMEM(near_mask.shape, jnp.int32),
            pltpu.SMEM(skeleton.shape, jnp.int32),
            pltpu.VMEM(box_inverse_parts.shape[1:], F32),
            pltpu.VMEM(near_coupling.shape[1:], F32),
            pltpu.VMEM((3, *top_inverse.shape[1:]), F32),
            pltpu.VMEM((2, rank, count), F32),
            pltpu.VMEM((2, len(OFFSETS), rank, count), F32),
            pltpu.VMEM((2, rank, count), F32),
            pltpu.VMEM((n_box, rank, count), F32),
            pltpu.VMEM((3, 2, rank, width), F32),
            pltpu.VMEM((2, 2, count // 2, width), F32),
            pltpu.VMEM((n_box // 2, 2, count // n_box, width), F32),
            pltpu.VMEM((2, 2, count // 2, width), F32),
            pltpu.VMEM((n_box // 2, 2, 2, count // n_box, width), F32),
            pltpu.VMEM((2, count // 2, width), F32),
            pltpu.VMEM((2, 3 * n_box // 2 * rank, 4 * width), BF16),
            pltpu.SemaphoreType.DMA((7,)),
            pltpu.SemaphoreType.DMA((2, len(OFFSETS))),
            pltpu.SemaphoreType.DMA((2, len(OFFSETS))),
            pltpu.SemaphoreType.DMA((n_box,)),
            pltpu.SemaphoreType.DMA((n_box,)),
            pltpu.SemaphoreType.DMA((2, 2)),
            pltpu.SemaphoreType.DMA((2, 2)),
            pltpu.SemaphoreType.DMA,
            pltpu.SemaphoreType.DMA,
            pltpu.SemaphoreType.DMA((n_box // 2,)),
            pltpu.SemaphoreType.DMA((n_box // 2,)),
            pltpu.SemaphoreType.DMA((n_box // 2,)),
            pltpu.SemaphoreType.DMA((n_box // 2,)),
        ],
        compiler_params=pltpu.CompilerParams(
            collective_id=0, has_side_effects=True, vmem_limit_bytes=16 * 1024 * 1024
        ),
    )(
        *(
            pltpu.with_memory_space_constraint(a, pltpu.HBM)
            for a in (
                surface_points,
                angle_ids.reshape(1, count),
                near_mask,
                skeleton,
                box_inverse_parts,
                near_coupling,
                top_inverse,
            )
        )
    )


def solution(mesh):
    return jax.shard_map(
        functools.partial(on_device, mesh.shape["blk"], mesh.shape["box"]),
        mesh=mesh,
        in_specs=(
            P(None, ("blk", "box")),
            P("batch"),
            P(("blk", "box"), None),
            P(("blk", "box"), None),
            P(("blk", "box"), None, None, None),
            P(("blk", "box"), None, None, None, None),
            P("blk", None, "box", None),
        ),
        out_specs=P(None, ("batch", "box"), "blk"),
        check_vma=False,
    )
```

```python
import functools

import jax
import jax.numpy as jnp
from jax import lax
from jax.experimental import pallas as pl
from jax.experimental.pallas import tpu as pltpu
from jax.sharding import PartitionSpec as P

SWEEP = 16384
WAVENUMBER = 24.0
OFFSETS = ((-1, -1), (-1, 0), (-1, 1), (0, -1), (0, 1), (1, -1), (1, 0), (1, 1))
MESH = pl.DeviceIdType.MESH
F32 = jnp.float32
BF16 = jnp.bfloat16


def sin_cos(x):
    n = jnp.round(x * (2.0 / jnp.pi))
    r = x - n * 1.5703125
    r = r - n * 4.8375129699707031e-4
    r = r - n * 7.5497899548918822e-8
    s = r * r
    sine = ((-1.9515295891e-4 * s + 8.3321608736e-3) * s - 1.6666654611e-1) * s * r + r
    cosine = ((2.443315711809948e-5 * s - 1.388731625493765e-3) * s + 4.166664568298827e-2) * (
        s * s
    ) + (1.0 - 0.5 * s)
    place = n - 4.0 * jnp.floor(n * 0.25)
    odd = (place == 1.0) | (place == 3.0)
    sin_sign = jnp.where(place >= 2.0, -1.0, 1.0)
    cos_sign = jnp.where((place == 1.0) | (place == 2.0), -1.0, 1.0)
    return sin_sign * jnp.where(odd, cosine, sine), cos_sign * jnp.where(odd, sine, cosine)


def split(x):
    high = x.astype(BF16)
    return high, (x - high.astype(F32)).astype(BF16)


def dot(a, b):
    return jnp.dot(a, b, preferred_element_type=F32)


def tall(a):
    return jnp.concatenate(a, axis=0)


def wide(b):
    return jnp.concatenate(b, axis=1)


def product(a, b):
    m, n = a.shape[0] // 2, b.shape[1] // 2
    c = dot(a, b)
    return c[:m, :n] + (c[:m, n:] + c[m:, :n])


def deep_left(a):
    high, low = split(a)
    return jnp.concatenate([high, low, high], axis=1)


def deep_right(b):
    high, low = split(b)
    return jnp.concatenate([high, high, low], axis=0)


def kernel(
    n_blk,
    n_box,
    points_hbm,
    angles_hbm,
    mask_hbm,
    skeleton_hbm,
    l_hbm,
    e_hbm,
    g_hbm,
    out_ref,
    points_ref,
    angles_ref,
    mask_ref,
    skeleton_ref,
    l_ref,
    e_ref,
    g_ref,
    u_ref,
    near_ref,
    mine_ref,
    t_ref,
    p_ref,
    above_ref,
    other_ref,
    x_ref,
    came_ref,
    held_ref,
    joined_ref,
    load_sem,
    u_send,
    u_recv,
    t_send,
    t_recv,
    pair_send,
    pair_recv,
    own_send,
    own_recv,
    w_send,
    w_recv,
    x_send,
    x_recv,
):
    r = lax.axis_index("blk")
    q = lax.axis_index("box")
    width = l_ref.shape[1]
    rank = u_ref.shape[1]
    count = u_ref.shape[2]
    share = count // n_box
    half = count // 2
    pairs = n_box // 2
    pair = q // 2
    side = lax.rem(q, 2)
    mate = r + 1 - 2 * lax.rem(r, 2)
    beyond = lax.rem(r - 1 + 2 * lax.rem(r, 2) + n_blk, n_blk)

    def around(dr, dq):
        return {"blk": lax.rem(r + dr + n_blk, n_blk), "box": lax.rem(q + dq + n_box, n_box)}

    def across(k):
        place = q
        bit = 1
        while bit <= k:
            if k & bit:
                place = place + bit - 2 * bit * lax.rem(q // bit, 2)
            bit *= 2
        return {"blk": mate, "box": place}

    loads = [
        pltpu.make_async_copy(angles_hbm, angles_ref, load_sem.at[0]),
        pltpu.make_async_copy(points_hbm, points_ref, load_sem.at[1]),
        pltpu.make_async_copy(l_hbm.at[0], l_ref, load_sem.at[2]),
        pltpu.make_async_copy(e_hbm.at[0], e_ref, load_sem.at[3]),
        pltpu.make_async_copy(skeleton_hbm, skeleton_ref, load_sem.at[5]),
        pltpu.make_async_copy(mask_hbm, mask_ref, load_sem.at[6]),
        pltpu.make_async_copy(g_hbm.at[0], g_ref.at[0], load_sem.at[4]),
    ]
    for load in loads:
        load.start()

    barrier = pltpu.get_barrier_semaphore()
    greeted = [around(0, d) for d in range(1, n_box)]
    greeted += [{"blk": mate, "box": to} for to in range(n_box)]
    greeted += [{"blk": beyond, "box": around(0, dq)["box"]} for dq in (-1, 0, 1)]
    for device in greeted:
        pl.semaphore_signal(barrier, inc=1, device_id=device, device_id_type=MESH)

    loads[0].wait()
    loads[1].wait()
    given = angles_ref[...].astype(F32)
    block = lax.broadcasted_iota(jnp.int32, (1, count), 1) // share
    theta = given
    for j in range(n_box):
        source = 2 * j if j < pairs else 2 * (j - pairs) + 1
        if source != j:
            moved = pltpu.roll(given, (j - source) % n_box * share, 1)
            theta = jnp.where(block == j, moved, theta)
    theta = theta * (2.0 * jnp.pi / SWEEP)
    sin_theta, cos_theta = sin_cos(theta)

    def column(i):
        return jnp.broadcast_to(points_ref[i : i + 1, :], (count, width)).T

    phase = WAVENUMBER * (
        column(0) * cos_theta + column(1) * (0.6 * sin_theta) + column(2) * (0.8 * sin_theta)
    )
    sine, cosine = sin_cos(phase)

    first = lax.broadcasted_iota(jnp.int32, (1, count), 1) < half

    def turned(a):
        return jnp.where(first, -1.0, 1.0) * pltpu.roll(a, half, 1)

    def complex_of(a):
        m = a.shape[0] // 2
        return a[:m] + turned(a[m:])

    def transposed_of(a):
        re, im = a[:, :width], a[:, width:]
        return jnp.stack([re[:half] - im[half:], re[half:] + im[:half]])

    field = [
        wide(split(jnp.where(first, cosine, pltpu.roll(sine, half, 1)))),
        wide(split(jnp.where(first, pltpu.roll(cosine, half, 1), sine))),
    ]

    loads[4].wait()
    row = lax.broadcasted_iota(jnp.int32, (rank, width), 0)
    lane = lax.broadcasted_iota(jnp.int32, (rank, width), 1)
    wanted = jnp.zeros((rank, width), jnp.int32)
    for k in range(rank):
        wanted = jnp.where(row == k, skeleton_ref[0, k], wanted)
    picker = jnp.where(wanted == lane, 1.0, 0.0).astype(BF16)

    def pick(a):
        return tuple(dot(picker, part).astype(BF16) for part in a)

    loads[2].wait()
    lr, li = split(l_ref[0]), split(l_ref[1])
    plr, pli = pick(lr), pick(li)
    picked = tall([plr[0], pli[0], plr[1], pli[1]])
    u = [complex_of(product(picked, part)) for part in field]
    for h in range(2):
        u_ref[h] = u[h]
    for i, part in enumerate((plr, pli)):
        p_ref[0, i] = part[0].astype(F32) + part[1].astype(F32)

    pl.semaphore_wait(barrier, len(greeted))

    u_copies = [[], []]
    for h in range(2):
        for m, (dr, dq) in enumerate(OFFSETS):
            copy = pltpu.make_async_remote_copy(
                src_ref=u_ref.at[h],
                dst_ref=near_ref.at[h, 7 - m],
                send_sem=u_send.at[h, m],
                recv_sem=u_recv.at[h, 7 - m],
                device_id=around(dr, dq),
                device_id_type=MESH,
            )
            copy.start()
            u_copies[h].append(copy)

    pair_copies = [
        pltpu.make_async_remote_copy(
            src_ref=ref.at[0],
            dst_ref=ref.at[1 + d],
            send_sem=pair_send.at[i, d],
            recv_sem=pair_recv.at[i, d],
            device_id=across(d),
            device_id_type=MESH,
        )
        for d in (1, 0)
        for i, ref in enumerate((g_ref, p_ref))
    ]
    loads[6].wait()
    for copy in pair_copies:
        copy.start()

    whole = tall([lr[0], li[0], lr[1], li[1]])
    z = [complex_of(product(whole, part)) for part in field]
    loads[3].wait()
    loads[5].wait()
    masked = [
        e_ref[m] * mask_ref[0, m].astype(F32) for m in range(len(OFFSETS))
    ]
    er = split(jnp.concatenate([e[0] for e in masked], axis=0).T)
    ei = split(jnp.concatenate([e[1] for e in masked], axis=0).T)
    per, pei = pick(er), pick(ei)
    coupling = tall([er[0], ei[0], er[1], ei[1]])
    picked_coupling = tall([per[0], pei[0], per[1], pei[1]])

    def send_t(h, d):
        return pltpu.make_async_remote_copy(
            src_ref=mine_ref.at[h],
            dst_ref=t_ref.at[q],
            send_sem=t_send.at[d],
            recv_sem=t_recv.at[d],
            device_id=across(d),
            device_id_type=MESH,
        )

    near = []
    for h in range(2):
        for copy in u_copies[h]:
            copy.wait_recv()
        near.append(wide(split(near_ref[h].reshape(len(OFFSETS) * rank, count))))
        mine_ref[h] = u[h] - complex_of(product(picked_coupling, near[h]))
        for d in (*sorted(range(2, n_box, 2), key=lambda d: (d.bit_count(), -d)), *range(n_box - 1, 0, -2), 0):

            @pl.when(lax.rem(q + d, 2) == h)
            def _(h=h, d=d):
                send_t(h, d).start()

    below = deep_right(jnp.concatenate([l_ref[0], l_ref[1]], axis=1))
    for h in range(2):
        w = z[h] - complex_of(product(coupling, near[h]))
        above_ref[h] = transposed_of(dot(deep_left(w.T), below))

    def send_w(to):
        return pltpu.make_async_remote_copy(
            src_ref=above_ref.at[1 - side, :, pl.ds(to * share, share)],
            dst_ref=other_ref.at[pair],
            send_sem=w_send.at[to],
            recv_sem=w_recv.at[pair],
            device_id={"blk": r, "box": 2 * to + 1 - side},
            device_id_type=MESH,
        )

    own_half = pltpu.make_async_remote_copy(
        src_ref=above_ref.at[side],
        dst_ref=held_ref,
        send_sem=own_send,
        recv_sem=own_recv,
        device_id=across(0),
        device_id_type=MESH,
    )
    own_half.start()
    for to in range(pairs):
        send_w(to).start()

    for copy in pair_copies:
        copy.wait_recv()
    joined = jnp.concatenate(
        [
            dot(
                deep_left(jnp.concatenate([g_ref[i, 0], g_ref[i, 1]], axis=0).T),
                deep_right(
                    jnp.concatenate(
                        [
                            jnp.concatenate([p_ref[i, 0], p_ref[i, 1]], axis=1),
                            jnp.concatenate([-p_ref[i, 1], p_ref[i, 0]], axis=1),
                        ],
                        axis=0,
                    )
                ),
            )
            for i in (1, 2)
        ],
        axis=1,
    )
    depth = pairs * rank
    for g in range(2):
        joined_ref[g] = deep_right(joined[g * depth : (g + 1) * depth])

    def part_of_x(g):
        t = t_ref[pl.ds(g * pairs, pairs)].reshape(depth, count)
        return dot(deep_left(t.T), joined_ref[g])

    near_half = q // pairs
    for d in range(pairs):
        send_t(0, d).wait_recv()
    x = part_of_x(near_half)
    own_half.wait_recv()
    for d in range(pairs, n_box):
        send_t(0, d).wait_recv()
    x = x + part_of_x(1 - near_half)
    x_ref[0] = held_ref[...] + transposed_of(x[:, : 2 * width])
    x_ref[1] = transposed_of(x[:, 2 * width :])

    def send_x(to, here):
        return pltpu.make_async_remote_copy(
            src_ref=x_ref.at[:, :, pl.ds(to * share, share)],
            dst_ref=came_ref.at[here],
            send_sem=x_send.at[to],
            recv_sem=x_recv.at[here],
            device_id={"blk": mate, "box": 2 * to + side},
            device_id_type=MESH,
        )

    for to in (0, *range(pairs - 1, 0, -1)):
        send_x(to, pair).start()

    def place(box):
        return pl.ds(pl.multiple_of(box * width, width), width)

    for here in range(pairs):
        pltpu.make_async_remote_copy(
            src_ref=above_ref.at[0, :, pl.ds(0, share)],
            dst_ref=other_ref.at[here],
            send_sem=w_send.at[here],
            recv_sem=w_recv.at[here],
            device_id=across(1),
            device_id_type=MESH,
        ).wait_recv()

    for here in range(pairs):
        send_x(here, here).wait_recv()
        out_ref[:, :, place(2 * here + side)] = came_ref[here, 0]
        out_ref[:, :, place(2 * here + 1 - side)] = came_ref[here, 1] + other_ref[here]

    for copy in u_copies[0] + u_copies[1] + pair_copies:
        copy.wait_send()
    own_half.wait_send()
    for d in range(n_box):
        send_t(0, d).wait_send()
    for to in range(pairs):
        send_w(to).wait_send()
        send_x(to, pair).wait_send()


def on_device(
    n_blk,
    n_box,
    surface_points,
    angle_ids,
    near_mask,
    skeleton,
    box_inverse_parts,
    near_coupling,
    top_inverse,
):
    width = box_inverse_parts.shape[2]
    count = angle_ids.shape[0]
    rank = skeleton.shape[1]
    vmem = pl.BlockSpec(memory_space=pltpu.VMEM)
    hbm = pl.BlockSpec(memory_space=pl.ANY)
    return pl.pallas_call(
        functools.partial(kernel, n_blk, n_box),
        out_shape=jax.ShapeDtypeStruct((2, count // n_box, n_box * width), F32),
        in_specs=[hbm] * 7,
        out_specs=vmem,
        scratch_shapes=[
            pltpu.VMEM(surface_points.shape, F32),
            pltpu.VMEM((1, count), jnp.int32),
            pltpu.SMEM(near_mask.shape, jnp.int32),
            pltpu.SMEM(skeleton.shape, jnp.int32),
            pltpu.VMEM(box_inverse_parts.shape[1:], F32),
            pltpu.VMEM(near_coupling.shape[1:], F32),
            pltpu.VMEM((3, *top_inverse.shape[1:]), F32),
            pltpu.VMEM((2, rank, count), F32),
            pltpu.VMEM((2, len(OFFSETS), rank, count), F32),
            pltpu.VMEM((2, rank, count), F32),
            pltpu.VMEM((n_box, rank, count), F32),
            pltpu.VMEM((3, 2, rank, width), F32),
            pltpu.VMEM((2, 2, count // 2, width), F32),
            pltpu.VMEM((n_box // 2, 2, count // n_box, width), F32),
            pltpu.VMEM((2, 2, count // 2, width), F32),
            pltpu.VMEM((n_box // 2, 2, 2, count // n_box, width), F32),
            pltpu.VMEM((2, count // 2, width), F32),
            pltpu.VMEM((2, 3 * n_box // 2 * rank, 4 * width), BF16),
            pltpu.SemaphoreType.DMA((7,)),
            pltpu.SemaphoreType.DMA((2, len(OFFSETS))),
            pltpu.SemaphoreType.DMA((2, len(OFFSETS))),
            pltpu.SemaphoreType.DMA((n_box,)),
            pltpu.SemaphoreType.DMA((n_box,)),
            pltpu.SemaphoreType.DMA((2, 2)),
            pltpu.SemaphoreType.DMA((2, 2)),
            pltpu.SemaphoreType.DMA,
            pltpu.SemaphoreType.DMA,
            pltpu.SemaphoreType.DMA((n_box // 2,)),
            pltpu.SemaphoreType.DMA((n_box // 2,)),
            pltpu.SemaphoreType.DMA((n_box // 2,)),
            pltpu.SemaphoreType.DMA((n_box // 2,)),
        ],
        compiler_params=pltpu.CompilerParams(
            collective_id=0, has_side_effects=True, vmem_limit_bytes=16 * 1024 * 1024
        ),
    )(
        *(
            pltpu.with_memory_space_constraint(a, pltpu.HBM)
            for a in (
                surface_points,
                angle_ids.reshape(1, count),
                near_mask,
                skeleton,
                box_inverse_parts,
                near_coupling,
                top_inverse,
            )
        )
    )


def solution(mesh):
    return jax.shard_map(
        functools.partial(on_device, mesh.shape["blk"], mesh.shape["box"]),
        mesh=mesh,
        in_specs=(
            P(None, ("blk", "box")),
            P("batch"),
            P(("blk", "box"), None),
            P(("blk", "box"), None),
            P(("blk", "box"), None, None, None),
            P(("blk", "box"), None, None, None, None),
            P("blk", None, "box", None),
        ),
        out_specs=P(None, ("batch", "box"), "blk"),
        check_vma=False,
    )
```

```python
import functools

import jax
import jax.numpy as jnp
from jax import lax
from jax.experimental import pallas as pl
from jax.experimental.pallas import tpu as pltpu
from jax.sharding import PartitionSpec as P

SWEEP = 16384
WAVENUMBER = 24.0
OFFSETS = ((-1, -1), (-1, 0), (-1, 1), (0, -1), (0, 1), (1, -1), (1, 0), (1, 1))
MESH = pl.DeviceIdType.MESH
F32 = jnp.float32
BF16 = jnp.bfloat16


def sin_cos(x):
    n = jnp.round(x * (2.0 / jnp.pi))
    r = x - n * 1.5703125
    r = r - n * 4.8375129699707031e-4
    r = r - n * 7.5497899548918822e-8
    s = r * r
    sine = ((-1.9515295891e-4 * s + 8.3321608736e-3) * s - 1.6666654611e-1) * s * r + r
    cosine = ((2.443315711809948e-5 * s - 1.388731625493765e-3) * s + 4.166664568298827e-2) * (
        s * s
    ) + (1.0 - 0.5 * s)
    place = n - 4.0 * jnp.floor(n * 0.25)
    odd = (place == 1.0) | (place == 3.0)
    sin_sign = jnp.where(place >= 2.0, -1.0, 1.0)
    cos_sign = jnp.where((place == 1.0) | (place == 2.0), -1.0, 1.0)
    return sin_sign * jnp.where(odd, cosine, sine), cos_sign * jnp.where(odd, sine, cosine)


def split(x):
    high = x.astype(BF16)
    return high, (x - high.astype(F32)).astype(BF16)


def dot(a, b):
    return jnp.dot(a, b, preferred_element_type=F32)


def tall(a):
    return jnp.concatenate(a, axis=0)


def wide(b):
    return jnp.concatenate(b, axis=1)


def product(a, b):
    m, n = a.shape[0] // 2, b.shape[1] // 2
    c = dot(a, b)
    return c[:m, :n] + (c[:m, n:] + c[m:, :n])


def deep_left(a):
    high, low = split(a)
    return jnp.concatenate([high, low, high], axis=1)


def deep_right(b):
    high, low = split(b)
    return jnp.concatenate([high, high, low], axis=0)


def kernel(
    n_blk,
    n_box,
    points_hbm,
    angles_hbm,
    mask_hbm,
    skeleton_hbm,
    l_hbm,
    e_hbm,
    g_hbm,
    out_ref,
    points_ref,
    angles_ref,
    mask_ref,
    skeleton_ref,
    l_ref,
    e_ref,
    g_ref,
    u_ref,
    near_ref,
    mine_ref,
    t_ref,
    p_ref,
    above_ref,
    other_ref,
    x_ref,
    came_ref,
    held_ref,
    joined_ref,
    load_sem,
    u_send,
    u_recv,
    t_send,
    t_recv,
    pair_send,
    pair_recv,
    own_send,
    own_recv,
    w_send,
    w_recv,
    x_send,
    x_recv,
):
    r = lax.axis_index("blk")
    q = lax.axis_index("box")
    width = l_ref.shape[1]
    rank = u_ref.shape[1]
    count = u_ref.shape[2]
    share = count // n_box
    half = count // 2
    pairs = n_box // 2
    pair = q // 2
    side = lax.rem(q, 2)
    mate = r + 1 - 2 * lax.rem(r, 2)
    beyond = lax.rem(r - 1 + 2 * lax.rem(r, 2) + n_blk, n_blk)

    def around(dr, dq):
        return {"blk": lax.rem(r + dr + n_blk, n_blk), "box": lax.rem(q + dq + n_box, n_box)}

    def across(k):
        place = q
        bit = 1
        while bit <= k:
            if k & bit:
                place = place + bit - 2 * bit * lax.rem(q // bit, 2)
            bit *= 2
        return {"blk": mate, "box": place}

    loads = [
        pltpu.make_async_copy(angles_hbm, angles_ref, load_sem.at[0]),
        pltpu.make_async_copy(points_hbm, points_ref, load_sem.at[1]),
        pltpu.make_async_copy(l_hbm.at[0], l_ref, load_sem.at[2]),
        pltpu.make_async_copy(e_hbm.at[0], e_ref, load_sem.at[3]),
        pltpu.make_async_copy(skeleton_hbm, skeleton_ref, load_sem.at[5]),
        pltpu.make_async_copy(mask_hbm, mask_ref, load_sem.at[6]),
    ]
    for load in loads:
        load.start()

    barrier = pltpu.get_barrier_semaphore()
    greeted = [around(0, d) for d in range(1, n_box)]
    greeted += [{"blk": mate, "box": to} for to in range(n_box)]
    greeted += [{"blk": beyond, "box": around(0, dq)["box"]} for dq in (-1, 0, 1)]
    for device in greeted:
        pl.semaphore_signal(barrier, inc=1, device_id=device, device_id_type=MESH)

    loads[0].wait()
    loads[1].wait()
    given = angles_ref[...].astype(F32)
    block = lax.broadcasted_iota(jnp.int32, (1, count), 1) // share
    theta = given
    for j in range(n_box):
        source = 2 * j if j < pairs else 2 * (j - pairs) + 1
        if source != j:
            moved = pltpu.roll(given, (j - source) % n_box * share, 1)
            theta = jnp.where(block == j, moved, theta)
    theta = theta * (2.0 * jnp.pi / SWEEP)
    sin_theta, cos_theta = sin_cos(theta)

    def column(i):
        return jnp.broadcast_to(points_ref[i : i + 1, :], (count, width)).T

    phase = WAVENUMBER * (
        column(0) * cos_theta + column(1) * (0.6 * sin_theta) + column(2) * (0.8 * sin_theta)
    )
    sine, cosine = sin_cos(phase)

    first = lax.broadcasted_iota(jnp.int32, (1, count), 1) < half

    def turned(a):
        return jnp.where(first, -1.0, 1.0) * pltpu.roll(a, half, 1)

    def complex_of(a):
        m = a.shape[0] // 2
        return a[:m] + turned(a[m:])

    def transposed_of(a):
        re, im = a[:, :width], a[:, width:]
        return jnp.stack([re[:half] - im[half:], re[half:] + im[:half]])

    field = [
        wide(split(jnp.where(first, cosine, pltpu.roll(sine, half, 1)))),
        wide(split(jnp.where(first, pltpu.roll(cosine, half, 1), sine))),
    ]

    loads[4].wait()
    row = lax.broadcasted_iota(jnp.int32, (rank, width), 0)
    lane = lax.broadcasted_iota(jnp.int32, (rank, width), 1)
    wanted = jnp.zeros((rank, width), jnp.int32)
    for k in range(rank):
        wanted = jnp.where(row == k, skeleton_ref[0, k], wanted)
    picker = jnp.where(wanted == lane, 1.0, 0.0).astype(BF16)

    def pick(a):
        return tuple(dot(picker, part).astype(BF16) for part in a)

    loads[2].wait()
    lr, li = split(l_ref[0]), split(l_ref[1])
    plr, pli = pick(lr), pick(li)
    picked = tall([plr[0], pli[0], plr[1], pli[1]])
    u = [complex_of(product(picked, part)) for part in field]
    for h in range(2):
        u_ref[h] = u[h]
    for i, part in enumerate((plr, pli)):
        p_ref[0, i] = part[0].astype(F32) + part[1].astype(F32)

    pl.semaphore_wait(barrier, len(greeted))

    u_copies = [[], []]
    for h in range(2):
        for m, (dr, dq) in enumerate(OFFSETS):
            copy = pltpu.make_async_remote_copy(
                src_ref=u_ref.at[h],
                dst_ref=near_ref.at[h, 7 - m],
                send_sem=u_send.at[h, m],
                recv_sem=u_recv.at[h, 7 - m],
                device_id=around(dr, dq),
                device_id_type=MESH,
            )
            copy.start()
            u_copies[h].append(copy)

    pair_copies = [
        pltpu.make_async_remote_copy(
            src_ref=source,
            dst_ref=ref.at[1 + d],
            send_sem=pair_send.at[i, d],
            recv_sem=pair_recv.at[i, d],
            device_id=across(d),
            device_id_type=MESH,
        )
        for d in (1, 0)
        for i, (source, ref) in enumerate(((g_hbm.at[0], g_ref), (p_ref.at[0], p_ref)))
    ]
    for copy in pair_copies:
        copy.start()

    whole = tall([lr[0], li[0], lr[1], li[1]])
    z = [complex_of(product(whole, part)) for part in field]
    loads[3].wait()
    loads[5].wait()
    masked = [
        e_ref[m] * mask_ref[0, m].astype(F32) for m in range(len(OFFSETS))
    ]
    er = split(jnp.concatenate([e[0] for e in masked], axis=0).T)
    ei = split(jnp.concatenate([e[1] for e in masked], axis=0).T)
    per, pei = pick(er), pick(ei)
    coupling = tall([er[0], ei[0], er[1], ei[1]])
    picked_coupling = tall([per[0], pei[0], per[1], pei[1]])

    def send_t(h, d):
        return pltpu.make_async_remote_copy(
            src_ref=mine_ref.at[h],
            dst_ref=t_ref.at[q],
            send_sem=t_send.at[d],
            recv_sem=t_recv.at[d],
            device_id=across(d),
            device_id_type=MESH,
        )

    near = []
    for h in range(2):
        for copy in u_copies[h]:
            copy.wait_recv()
        near.append(wide(split(near_ref[h].reshape(len(OFFSETS) * rank, count))))
        mine_ref[h] = u[h] - complex_of(product(picked_coupling, near[h]))
        for d in (*sorted(range(2, n_box, 2), key=lambda d: (d.bit_count(), -d)), *range(n_box - 1, 0, -2), 0):

            @pl.when(lax.rem(q + d, 2) == h)
            def _(h=h, d=d):
                send_t(h, d).start()

    below = deep_right(jnp.concatenate([l_ref[0], l_ref[1]], axis=1))
    for h in range(2):
        w = z[h] - complex_of(product(coupling, near[h]))
        above_ref[h] = transposed_of(dot(deep_left(w.T), below))

    def send_w(to):
        return pltpu.make_async_remote_copy(
            src_ref=above_ref.at[1 - side, :, pl.ds(to * share, share)],
            dst_ref=other_ref.at[pair],
            send_sem=w_send.at[to],
            recv_sem=w_recv.at[pair],
            device_id={"blk": r, "box": 2 * to + 1 - side},
            device_id_type=MESH,
        )

    own_half = pltpu.make_async_remote_copy(
        src_ref=above_ref.at[side],
        dst_ref=held_ref,
        send_sem=own_send,
        recv_sem=own_recv,
        device_id=across(0),
        device_id_type=MESH,
    )
    own_half.start()
    for to in range(pairs):
        send_w(to).start()

    for copy in pair_copies:
        copy.wait_recv()
    joined = jnp.concatenate(
        [
            dot(
                deep_left(jnp.concatenate([g_ref[i, 0], g_ref[i, 1]], axis=0).T),
                deep_right(
                    jnp.concatenate(
                        [
                            jnp.concatenate([p_ref[i, 0], p_ref[i, 1]], axis=1),
                            jnp.concatenate([-p_ref[i, 1], p_ref[i, 0]], axis=1),
                        ],
                        axis=0,
                    )
                ),
            )
            for i in (1, 2)
        ],
        axis=1,
    )
    depth = pairs * rank
    for g in range(2):
        joined_ref[g] = deep_right(joined[g * depth : (g + 1) * depth])

    def part_of_x(g):
        t = t_ref[pl.ds(g * pairs, pairs)].reshape(depth, count)
        return dot(deep_left(t.T), joined_ref[g])

    near_half = q // pairs
    for d in range(pairs):
        send_t(0, d).wait_recv()
    x = part_of_x(near_half)
    own_half.wait_recv()
    for d in range(pairs, n_box):
        send_t(0, d).wait_recv()
    x = x + part_of_x(1 - near_half)
    x_ref[0] = held_ref[...] + transposed_of(x[:, : 2 * width])
    x_ref[1] = transposed_of(x[:, 2 * width :])

    def send_x(to, here):
        return pltpu.make_async_remote_copy(
            src_ref=x_ref.at[:, :, pl.ds(to * share, share)],
            dst_ref=came_ref.at[here],
            send_sem=x_send.at[to],
            recv_sem=x_recv.at[here],
            device_id={"blk": mate, "box": 2 * to + side},
            device_id_type=MESH,
        )

    for to in (0, *range(pairs - 1, 0, -1)):
        send_x(to, pair).start()

    def place(box):
        return pl.ds(pl.multiple_of(box * width, width), width)

    for here in range(pairs):
        pltpu.make_async_remote_copy(
            src_ref=above_ref.at[0, :, pl.ds(0, share)],
            dst_ref=other_ref.at[here],
            send_sem=w_send.at[here],
            recv_sem=w_recv.at[here],
            device_id=across(1),
            device_id_type=MESH,
        ).wait_recv()

    for here in range(pairs):
        send_x(here, here).wait_recv()
        out_ref[:, :, place(2 * here + side)] = came_ref[here, 0]
        out_ref[:, :, place(2 * here + 1 - side)] = came_ref[here, 1] + other_ref[here]

    for copy in u_copies[0] + u_copies[1] + pair_copies:
        copy.wait_send()
    own_half.wait_send()
    for d in range(n_box):
        send_t(0, d).wait_send()
    for to in range(pairs):
        send_w(to).wait_send()
        send_x(to, pair).wait_send()


def on_device(
    n_blk,
    n_box,
    surface_points,
    angle_ids,
    near_mask,
    skeleton,
    box_inverse_parts,
    near_coupling,
    top_inverse,
):
    width = box_inverse_parts.shape[2]
    count = angle_ids.shape[0]
    rank = skeleton.shape[1]
    vmem = pl.BlockSpec(memory_space=pltpu.VMEM)
    hbm = pl.BlockSpec(memory_space=pl.ANY)
    return pl.pallas_call(
        functools.partial(kernel, n_blk, n_box),
        out_shape=jax.ShapeDtypeStruct((2, count // n_box, n_box * width), F32),
        in_specs=[hbm] * 7,
        out_specs=vmem,
        scratch_shapes=[
            pltpu.VMEM(surface_points.shape, F32),
            pltpu.VMEM((1, count), jnp.int32),
            pltpu.SMEM(near_mask.shape, jnp.int32),
            pltpu.SMEM(skeleton.shape, jnp.int32),
            pltpu.VMEM(box_inverse_parts.shape[1:], F32),
            pltpu.VMEM(near_coupling.shape[1:], F32),
            pltpu.VMEM((3, *top_inverse.shape[1:]), F32),
            pltpu.VMEM((2, rank, count), F32),
            pltpu.VMEM((2, len(OFFSETS), rank, count), F32),
            pltpu.VMEM((2, rank, count), F32),
            pltpu.VMEM((n_box, rank, count), F32),
            pltpu.VMEM((3, 2, rank, width), F32),
            pltpu.VMEM((2, 2, count // 2, width), F32),
            pltpu.VMEM((n_box // 2, 2, count // n_box, width), F32),
            pltpu.VMEM((2, 2, count // 2, width), F32),
            pltpu.VMEM((n_box // 2, 2, 2, count // n_box, width), F32),
            pltpu.VMEM((2, count // 2, width), F32),
            pltpu.VMEM((2, 3 * n_box // 2 * rank, 4 * width), BF16),
            pltpu.SemaphoreType.DMA((7,)),
            pltpu.SemaphoreType.DMA((2, len(OFFSETS))),
            pltpu.SemaphoreType.DMA((2, len(OFFSETS))),
            pltpu.SemaphoreType.DMA((n_box,)),
            pltpu.SemaphoreType.DMA((n_box,)),
            pltpu.SemaphoreType.DMA((2, 2)),
            pltpu.SemaphoreType.DMA((2, 2)),
            pltpu.SemaphoreType.DMA,
            pltpu.SemaphoreType.DMA,
            pltpu.SemaphoreType.DMA((n_box // 2,)),
            pltpu.SemaphoreType.DMA((n_box // 2,)),
            pltpu.SemaphoreType.DMA((n_box // 2,)),
            pltpu.SemaphoreType.DMA((n_box // 2,)),
        ],
        compiler_params=pltpu.CompilerParams(
            collective_id=0, has_side_effects=True, vmem_limit_bytes=16 * 1024 * 1024
        ),
    )(
        *(
            pltpu.with_memory_space_constraint(a, pltpu.HBM)
            for a in (
                surface_points,
                angle_ids.reshape(1, count),
                near_mask,
                skeleton,
                box_inverse_parts,
                near_coupling,
                top_inverse,
            )
        )
    )


def solution(mesh):
    return jax.shard_map(
        functools.partial(on_device, mesh.shape["blk"], mesh.shape["box"]),
        mesh=mesh,
        in_specs=(
            P(None, ("blk", "box")),
            P("batch"),
            P(("blk", "box"), None),
            P(("blk", "box"), None),
            P(("blk", "box"), None, None, None),
            P(("blk", "box"), None, None, None, None),
            P("blk", None, "box", None),
        ),
        out_specs=P(None, ("batch", "box"), "blk"),
        check_vma=False,
    )
```

```python
import functools

import jax
import jax.numpy as jnp
from jax import lax
from jax.experimental import pallas as pl
from jax.experimental.pallas import tpu as pltpu
from jax.sharding import PartitionSpec as P

SWEEP = 16384
WAVENUMBER = 24.0
OFFSETS = ((-1, -1), (-1, 0), (-1, 1), (0, -1), (0, 1), (1, -1), (1, 0), (1, 1))
MESH = pl.DeviceIdType.MESH
F32 = jnp.float32
BF16 = jnp.bfloat16


def sin_cos(x):
    n = jnp.round(x * (2.0 / jnp.pi))
    r = x - n * 1.5703125
    r = r - n * 4.8375129699707031e-4
    r = r - n * 7.5497899548918822e-8
    s = r * r
    sine = ((-1.9515295891e-4 * s + 8.3321608736e-3) * s - 1.6666654611e-1) * s * r + r
    cosine = ((2.443315711809948e-5 * s - 1.388731625493765e-3) * s + 4.166664568298827e-2) * (
        s * s
    ) + (1.0 - 0.5 * s)
    place = n - 4.0 * jnp.floor(n * 0.25)
    odd = (place == 1.0) | (place == 3.0)
    sin_sign = jnp.where(place >= 2.0, -1.0, 1.0)
    cos_sign = jnp.where((place == 1.0) | (place == 2.0), -1.0, 1.0)
    return sin_sign * jnp.where(odd, cosine, sine), cos_sign * jnp.where(odd, sine, cosine)


def split(x):
    high = x.astype(BF16)
    return high, (x - high.astype(F32)).astype(BF16)


def dot(a, b):
    return jnp.dot(a, b, preferred_element_type=F32)


def tall(a):
    return jnp.concatenate(a, axis=0)


def wide(b):
    return jnp.concatenate(b, axis=1)


def product(a, b):
    m, n = a.shape[0] // 2, b.shape[1] // 2
    c = dot(a, b)
    return c[:m, :n] + (c[:m, n:] + c[m:, :n])


def deep_left(a):
    high, low = split(a)
    return jnp.concatenate([high, low, high], axis=1)


def deep_right(b):
    high, low = split(b)
    return jnp.concatenate([high, high, low], axis=0)


def kernel(
    n_blk,
    n_box,
    points_hbm,
    angles_hbm,
    mask_hbm,
    skeleton_hbm,
    l_hbm,
    e_hbm,
    g_hbm,
    out_ref,
    points_ref,
    angles_ref,
    mask_ref,
    skeleton_ref,
    l_ref,
    e_ref,
    g_ref,
    u_ref,
    near_ref,
    mine_ref,
    t_ref,
    p_ref,
    above_ref,
    other_ref,
    x_ref,
    came_ref,
    held_ref,
    joined_ref,
    load_sem,
    u_send,
    u_recv,
    t_send,
    t_recv,
    pair_send,
    pair_recv,
    own_send,
    own_recv,
    w_send,
    w_recv,
    x_send,
    x_recv,
):
    r = lax.axis_index("blk")
    q = lax.axis_index("box")
    width = l_ref.shape[1]
    rank = u_ref.shape[1]
    count = u_ref.shape[2]
    share = count // n_box
    half = count // 2
    pairs = n_box // 2
    pair = q // 2
    side = lax.rem(q, 2)
    mate = r + 1 - 2 * lax.rem(r, 2)
    beyond = lax.rem(r - 1 + 2 * lax.rem(r, 2) + n_blk, n_blk)

    def around(dr, dq):
        return {"blk": lax.rem(r + dr + n_blk, n_blk), "box": lax.rem(q + dq + n_box, n_box)}

    def across(k):
        place = q
        bit = 1
        while bit <= k:
            if k & bit:
                place = place + bit - 2 * bit * lax.rem(q // bit, 2)
            bit *= 2
        return {"blk": mate, "box": place}

    loads = [
        pltpu.make_async_copy(angles_hbm, angles_ref, load_sem.at[0]),
        pltpu.make_async_copy(points_hbm, points_ref, load_sem.at[1]),
        pltpu.make_async_copy(l_hbm.at[0], l_ref, load_sem.at[2]),
        pltpu.make_async_copy(e_hbm.at[0], e_ref, load_sem.at[3]),
        pltpu.make_async_copy(skeleton_hbm, skeleton_ref, load_sem.at[5]),
        pltpu.make_async_copy(mask_hbm, mask_ref, load_sem.at[6]),
        pltpu.make_async_copy(g_hbm.at[0], g_ref.at[0], load_sem.at[4]),
    ]
    for load in loads:
        load.start()

    barrier = pltpu.get_barrier_semaphore()
    greeted = [around(0, d) for d in range(1, n_box)]
    greeted += [{"blk": mate, "box": to} for to in range(n_box)]
    greeted += [{"blk": beyond, "box": around(0, dq)["box"]} for dq in (-1, 0, 1)]
    for device in greeted:
        pl.semaphore_signal(barrier, inc=1, device_id=device, device_id_type=MESH)

    loads[0].wait()
    loads[1].wait()
    given = angles_ref[...].astype(F32)
    block = lax.broadcasted_iota(jnp.int32, (1, count), 1) // share
    theta = given
    for j in range(n_box):
        source = 2 * j if j < pairs else 2 * (j - pairs) + 1
        if source != j:
            moved = pltpu.roll(given, (j - source) % n_box * share, 1)
            theta = jnp.where(block == j, moved, theta)
    theta = theta * (2.0 * jnp.pi / SWEEP)
    sin_theta, cos_theta = sin_cos(theta)

    def column(i):
        return jnp.broadcast_to(points_ref[i : i + 1, :], (count, width)).T

    phase = WAVENUMBER * (
        column(0) * cos_theta + column(1) * (0.6 * sin_theta) + column(2) * (0.8 * sin_theta)
    )
    sine, cosine = sin_cos(phase)

    first = lax.broadcasted_iota(jnp.int32, (1, count), 1) < half

    def turned(a):
        return jnp.where(first, -1.0, 1.0) * pltpu.roll(a, half, 1)

    def complex_of(a):
        m = a.shape[0] // 2
        return a[:m] + turned(a[m:])

    def transposed_of(a):
        re, im = a[:, :width], a[:, width:]
        return jnp.stack([re[:half] - im[half:], re[half:] + im[:half]])

    field = [
        wide(split(jnp.where(first, cosine, pltpu.roll(sine, half, 1)))),
        wide(split(jnp.where(first, pltpu.roll(cosine, half, 1), sine))),
    ]

    loads[4].wait()
    row = lax.broadcasted_iota(jnp.int32, (rank, width), 0)
    lane = lax.broadcasted_iota(jnp.int32, (rank, width), 1)
    wanted = jnp.zeros((rank, width), jnp.int32)
    for k in range(rank):
        wanted = jnp.where(row == k, skeleton_ref[0, k], wanted)
    picker = jnp.where(wanted == lane, 1.0, 0.0).astype(BF16)

    def pick(a):
        return tuple(dot(picker, part).astype(BF16) for part in a)

    loads[2].wait()
    lr, li = split(l_ref[0]), split(l_ref[1])
    plr, pli = pick(lr), pick(li)
    picked = tall([plr[0], pli[0], plr[1], pli[1]])
    u = [complex_of(product(picked, part)) for part in field]
    for h in range(2):
        u_ref[h] = u[h]
    for i, part in enumerate((plr, pli)):
        p_ref[0, i] = part[0].astype(F32) + part[1].astype(F32)

    pl.semaphore_wait(barrier, len(greeted))

    u_copies = [[], []]
    for h in range(2):
        for m, (dr, dq) in enumerate(OFFSETS):
            copy = pltpu.make_async_remote_copy(
                src_ref=u_ref.at[h],
                dst_ref=near_ref.at[h, 7 - m],
                send_sem=u_send.at[h, m],
                recv_sem=u_recv.at[h, 7 - m],
                device_id=around(dr, dq),
                device_id_type=MESH,
            )
            copy.start()
            u_copies[h].append(copy)

    pair_copies = [
        pltpu.make_async_remote_copy(
            src_ref=ref.at[0],
            dst_ref=ref.at[1 + d],
            send_sem=pair_send.at[i, d],
            recv_sem=pair_recv.at[i, d],
            device_id=across(d),
            device_id_type=MESH,
        )
        for d in (1, 0)
        for i, ref in enumerate((g_ref, p_ref))
    ]
    loads[6].wait()
    for copy in pair_copies:
        copy.start()

    whole = tall([lr[0], li[0], lr[1], li[1]])
    z = [complex_of(product(whole, part)) for part in field]
    loads[3].wait()
    loads[5].wait()
    masked = [
        e_ref[m] * mask_ref[0, m].astype(F32) for m in range(len(OFFSETS))
    ]
    er = split(jnp.concatenate([e[0] for e in masked], axis=0).T)
    ei = split(jnp.concatenate([e[1] for e in masked], axis=0).T)
    per, pei = pick(er), pick(ei)
    coupling = tall([er[0], ei[0], er[1], ei[1]])
    picked_coupling = tall([per[0], pei[0], per[1], pei[1]])

    def send_t(h, d):
        return pltpu.make_async_remote_copy(
            src_ref=mine_ref.at[h],
            dst_ref=t_ref.at[q],
            send_sem=t_send.at[d],
            recv_sem=t_recv.at[d],
            device_id=across(d),
            device_id_type=MESH,
        )

    near = []
    for h in range(2):
        for copy in u_copies[h]:
            copy.wait_recv()
        near.append(wide(split(near_ref[h].reshape(len(OFFSETS) * rank, count))))
        mine_ref[h] = u[h] - complex_of(product(picked_coupling, near[h]))
        for e in (3, 2, 1, 0):
            pltpu.make_async_remote_copy(
                src_ref=mine_ref.at[h],
                dst_ref=t_ref.at[q],
                send_sem=t_send.at[2 * e + lax.rem(h + side, 2)],
                recv_sem=t_recv.at[2 * e + lax.rem(h + side, 2)],
                device_id={"blk": mate, "box": across(2 * e)["box"] - side + h},
                device_id_type=MESH,
            ).start()

    below = deep_right(jnp.concatenate([l_ref[0], l_ref[1]], axis=1))
    for h in range(2):
        w = z[h] - complex_of(product(coupling, near[h]))
        above_ref[h] = transposed_of(dot(deep_left(w.T), below))

    def send_w(to):
        return pltpu.make_async_remote_copy(
            src_ref=above_ref.at[1 - side, :, pl.ds(to * share, share)],
            dst_ref=other_ref.at[pair],
            send_sem=w_send.at[to],
            recv_sem=w_recv.at[pair],
            device_id={"blk": r, "box": 2 * to + 1 - side},
            device_id_type=MESH,
        )

    own_half = pltpu.make_async_remote_copy(
        src_ref=above_ref.at[side],
        dst_ref=held_ref,
        send_sem=own_send,
        recv_sem=own_recv,
        device_id=across(0),
        device_id_type=MESH,
    )
    own_half.start()
    for to in range(pairs):
        send_w(to).start()

    for copy in pair_copies:
        copy.wait_recv()
    joined = jnp.concatenate(
        [
            dot(
                deep_left(jnp.concatenate([g_ref[i, 0], g_ref[i, 1]], axis=0).T),
                deep_right(
                    jnp.concatenate(
                        [
                            jnp.concatenate([p_ref[i, 0], p_ref[i, 1]], axis=1),
                            jnp.concatenate([-p_ref[i, 1], p_ref[i, 0]], axis=1),
                        ],
                        axis=0,
                    )
                ),
            )
            for i in (1, 2)
        ],
        axis=1,
    )
    depth = pairs * rank
    for g in range(2):
        joined_ref[g] = deep_right(joined[g * depth : (g + 1) * depth])

    def part_of_x(g):
        t = t_ref[pl.ds(g * pairs, pairs)].reshape(depth, count)
        return dot(deep_left(t.T), joined_ref[g])

    near_half = q // pairs
    for d in range(pairs):
        send_t(0, d).wait_recv()
    x = part_of_x(near_half)
    own_half.wait_recv()
    for d in range(pairs, n_box):
        send_t(0, d).wait_recv()
    x = x + part_of_x(1 - near_half)
    x_ref[0] = held_ref[...] + transposed_of(x[:, : 2 * width])
    x_ref[1] = transposed_of(x[:, 2 * width :])

    def send_x(to, here):
        return pltpu.make_async_remote_copy(
            src_ref=x_ref.at[:, :, pl.ds(to * share, share)],
            dst_ref=came_ref.at[here],
            send_sem=x_send.at[to],
            recv_sem=x_recv.at[here],
            device_id={"blk": mate, "box": 2 * to + side},
            device_id_type=MESH,
        )

    for to in (0, *range(pairs - 1, 0, -1)):
        send_x(to, pair).start()

    def place(box):
        return pl.ds(pl.multiple_of(box * width, width), width)

    for here in range(pairs):
        pltpu.make_async_remote_copy(
            src_ref=above_ref.at[0, :, pl.ds(0, share)],
            dst_ref=other_ref.at[here],
            send_sem=w_send.at[here],
            recv_sem=w_recv.at[here],
            device_id=across(1),
            device_id_type=MESH,
        ).wait_recv()

    for here in range(pairs):
        send_x(here, here).wait_recv()
        out_ref[:, :, place(2 * here + side)] = came_ref[here, 0]
        out_ref[:, :, place(2 * here + 1 - side)] = came_ref[here, 1] + other_ref[here]

    for copy in u_copies[0] + u_copies[1] + pair_copies:
        copy.wait_send()
    own_half.wait_send()
    for d in range(n_box):
        send_t(0, d).wait_send()
    for to in range(pairs):
        send_w(to).wait_send()
        send_x(to, pair).wait_send()


def on_device(
    n_blk,
    n_box,
    surface_points,
    angle_ids,
    near_mask,
    skeleton,
    box_inverse_parts,
    near_coupling,
    top_inverse,
):
    width = box_inverse_parts.shape[2]
    count = angle_ids.shape[0]
    rank = skeleton.shape[1]
    vmem = pl.BlockSpec(memory_space=pltpu.VMEM)
    hbm = pl.BlockSpec(memory_space=pl.ANY)
    return pl.pallas_call(
        functools.partial(kernel, n_blk, n_box),
        out_shape=jax.ShapeDtypeStruct((2, count // n_box, n_box * width), F32),
        in_specs=[hbm] * 7,
        out_specs=vmem,
        scratch_shapes=[
            pltpu.VMEM(surface_points.shape, F32),
            pltpu.VMEM((1, count), jnp.int32),
            pltpu.SMEM(near_mask.shape, jnp.int32),
            pltpu.SMEM(skeleton.shape, jnp.int32),
            pltpu.VMEM(box_inverse_parts.shape[1:], F32),
            pltpu.VMEM(near_coupling.shape[1:], F32),
            pltpu.VMEM((3, *top_inverse.shape[1:]), F32),
            pltpu.VMEM((2, rank, count), F32),
            pltpu.VMEM((2, len(OFFSETS), rank, count), F32),
            pltpu.VMEM((2, rank, count), F32),
            pltpu.VMEM((n_box, rank, count), F32),
            pltpu.VMEM((3, 2, rank, width), F32),
            pltpu.VMEM((2, 2, count // 2, width), F32),
            pltpu.VMEM((n_box // 2, 2, count // n_box, width), F32),
            pltpu.VMEM((2, 2, count // 2, width), F32),
            pltpu.VMEM((n_box // 2, 2, 2, count // n_box, width), F32),
            pltpu.VMEM((2, count // 2, width), F32),
            pltpu.VMEM((2, 3 * n_box // 2 * rank, 4 * width), BF16),
            pltpu.SemaphoreType.DMA((7,)),
            pltpu.SemaphoreType.DMA((2, len(OFFSETS))),
            pltpu.SemaphoreType.DMA((2, len(OFFSETS))),
            pltpu.SemaphoreType.DMA((n_box,)),
            pltpu.SemaphoreType.DMA((n_box,)),
            pltpu.SemaphoreType.DMA((2, 2)),
            pltpu.SemaphoreType.DMA((2, 2)),
            pltpu.SemaphoreType.DMA,
            pltpu.SemaphoreType.DMA,
            pltpu.SemaphoreType.DMA((n_box // 2,)),
            pltpu.SemaphoreType.DMA((n_box // 2,)),
            pltpu.SemaphoreType.DMA((n_box // 2,)),
            pltpu.SemaphoreType.DMA((n_box // 2,)),
        ],
        compiler_params=pltpu.CompilerParams(
            collective_id=0, has_side_effects=True, vmem_limit_bytes=16 * 1024 * 1024
        ),
    )(
        *(
            pltpu.with_memory_space_constraint(a, pltpu.HBM)
            for a in (
                surface_points,
                angle_ids.reshape(1, count),
                near_mask,
                skeleton,
                box_inverse_parts,
                near_coupling,
                top_inverse,
            )
        )
    )


def solution(mesh):
    return jax.shard_map(
        functools.partial(on_device, mesh.shape["blk"], mesh.shape["box"]),
        mesh=mesh,
        in_specs=(
            P(None, ("blk", "box")),
            P("batch"),
            P(("blk", "box"), None),
            P(("blk", "box"), None),
            P(("blk", "box"), None, None, None),
            P(("blk", "box"), None, None, None, None),
            P("blk", None, "box", None),
        ),
        out_specs=P(None, ("batch", "box"), "blk"),
        check_vma=False,
    )
```
